128 devices in a mesh: pos: 64 (over y, x_hi, z, core), frame: 2 (over x_lo).
Axes of the slice: x: 4 (x_hi: 2, x_lo: 2; x = x_hi * 2 + x_lo), y: 4, z: 4, core: 2. Of those that a mesh axis runs over, the one named last changes fastest.
Arguments:
- tokens: bfloat16 [8, 16, 256, 768], P('frame', None, 'pos'), may hold values from -6 to 6
- modulation: float32 [8, 2, 2, 6, 768], P('frame'), may hold values from -3 to 3
- box_bounds: int32 [8, 6], P('frame'), may hold values from 0 to 16, as said below
- masters: float32 [896, 128, 128], P('pos')
- left_stats: float32 [896, 128, 128], P('pos'), as said below
- right_stats: float32 [896, 128, 128], P('pos'), as said below
- left_roots: float32 [896, 128, 128], P('pos'), as said below
- right_roots: float32 [896, 128, 128], P('pos'), as said below
- owner_slot: int32 [864], replicated, may hold values from 0 to 895, as said below
- cotangent: bfloat16 [8, 16, 256, 768], P('frame', None, 'pos'), may hold values from -6 to 6
Outputs:
- block_output: bfloat16 [8, 16, 256, 768], P('frame', None, 'pos')
- token_grads: bfloat16 [8, 16, 256, 768], P('frame', None, 'pos')
- tile_grads: float32 [896, 128, 128], P('pos')
- new_left: float32 [896, 128, 128], P('pos')
- new_right: float32 [896, 128, 128], P('pos')
- new_masters: float32 [896, 128, 128], P('pos')
The draws below stay inside these ranges and needn't reach their ends.
Inputs may be any that keep to these rules, and one draw needn't show every extreme that they name: Distinct slots: tile t of the weights is held at slot owner_slot[t]; the other 32 slots hold no tile. For each clip c: box_bounds[c, 0] < box_bounds[c, 1] <= 16, box_bounds[c, 2] < box_bounds[c, 3] <= 16, box_bounds[c, 4] < box_bounds[c, 5] <= 16. `left_stats`: each slot's matrix is symmetric positive definite. `right_stats`: each slot's matrix is symmetric positive definite. `left_roots`: each slot's matrix is symmetric positive definite. `right_roots`: each slot's matrix is symmetric positive definite.
All inputs are finite; a program needn't handle non-finite values.
Results may differ from the reference program's by a relative error of at most 0.015.
Values may be sent and summed in bfloat16 or wider, within the bound.
No kernel may reach another device: no remote copies, remote signals or barrier semaphores. Data moves between devices by JAX's collectives and lax.ppermute only.
A program may use at most 320 MiB of HBM per device.

```python
import jax
import jax.numpy as jnp
import numpy as np
from jax import lax

D = 768
HEADS = 12
HD = 64
FF = 3072
FRAMES = 16
GRID = 16
BLOCK = 128
PATCHES = 256
CLIPS = 8
TILES = 864
SLOTS = 896


def owner_table(seed_key):
    seed_key = jax.random.fold_in(seed_key, 71)
    key_inner, key_order = jax.random.split(seed_key)
    inner_slots = 1 + jax.random.permutation(key_inner, SLOTS - 2)[:TILES - 2]
    chosen = jnp.concatenate([jnp.zeros((1,), jnp.int32), inner_slots.astype(jnp.int32), jnp.full((1,), SLOTS - 1, jnp.int32)])
    return chosen[jax.random.permutation(key_order, TILES)]


def tile_scales():
    master_std = []
    grad_size = []
    token_total = CLIPS * FRAMES * PATCHES
    for keys_count in (PATCHES, FRAMES):
        out_std = (keys_count / 27.0) ** 0.5 * D ** (-0.5)
        out_grad = 0.8 * min(1.0, (18.0 / keys_count) ** 0.5)
        for row_count, col_count, weight_std, grad_rms in ((D, 3 * D, D ** (-0.5), 0.5), (D, D, out_std, out_grad), (D, FF, D ** (-0.5), 0.24), (FF, D, FF ** (-0.5), 0.54)):
            tile_count = row_count // BLOCK * (col_count // BLOCK)
            master_std += [weight_std] * tile_count
            grad_size += [grad_rms * token_total ** 0.5] * tile_count
    return (np.array(master_std, np.float32), np.array(grad_size, np.float32))


def slot_params(seed_key):
    owners = owner_table(seed_key)
    master_std, grad_size = tile_scales()
    slot_tile = jnp.zeros((SLOTS,), jnp.int32).at[owners].set(jnp.arange(TILES, dtype=jnp.int32))
    return (jnp.asarray(master_std)[slot_tile], jnp.asarray(grad_size)[slot_tile])


def symmetric(seed_key, spread):
    normal_base = jax.random.normal(seed_key, (SLOTS, BLOCK, BLOCK), jnp.float32)
    return (normal_base + jnp.swapaxes(normal_base, 1, 2)) * 0.5 ** 0.5 * spread[:, None, None]


def statistic(seed_key, grad_size):
    key_diag, key_off = jax.random.split(seed_key)
    diagonal = jax.random.uniform(key_diag, (SLOTS, BLOCK), jnp.float32, 1.0, 4.0) * (BLOCK * grad_size * grad_size)[:, None]
    identity = jnp.eye(BLOCK, dtype=jnp.float32)
    return diagonal[:, :, None] * identity + symmetric(key_off, 0.25 * BLOCK ** 0.5 * grad_size * grad_size)


def inverse_root(seed_key, grad_size):
    key_diag, key_off = jax.random.split(seed_key)
    factor = (2.5 * BLOCK * grad_size * grad_size) ** (-0.25)
    diagonal = jax.random.uniform(key_diag, (SLOTS, BLOCK), jnp.float32, 0.7, 1.4)
    identity = jnp.eye(BLOCK, dtype=jnp.float32)
    off_diagonal = symmetric(key_off, jnp.full((SLOTS,), 0.3 * BLOCK ** (-0.5), jnp.float32))
    return factor[:, None, None] * (diagonal[:, :, None] * identity + off_diagonal)


def draw_owner_slot(key, part):
    return owner_table(key)


def draw_masters(key, part):
    master_std, grad_size = slot_params(key)
    key = jax.random.fold_in(key, 3)
    return master_std[:, None, None] * jax.random.normal(key, (SLOTS, BLOCK, BLOCK), jnp.float32)


def draw_left_stats(key, part):
    master_std, grad_size = slot_params(key)
    key = jax.random.fold_in(key, 5)
    return statistic(key, grad_size)


def draw_right_stats(key, part):
    master_std, grad_size = slot_params(key)
    key = jax.random.fold_in(key, 7)
    return statistic(key, grad_size)


def draw_left_roots(key, part):
    master_std, grad_size = slot_params(key)
    key = jax.random.fold_in(key, 11)
    return inverse_root(key, grad_size)


def draw_right_roots(key, part):
    master_std, grad_size = slot_params(key)
    key = jax.random.fold_in(key, 13)
    return inverse_root(key, grad_size)


def draw_box_bounds(key, part):
    key = jax.random.fold_in(key, 17)
    pieces = []
    for index_key, extent in zip(jax.random.split(key, 3), (FRAMES, GRID, GRID)):
        key_low, key_high = jax.random.split(index_key)
        lower_raw = jax.random.randint(key_low, (CLIPS,), 0, extent // 2)
        upper_raw = jax.random.randint(key_high, (CLIPS,), 0, extent // 2)
        pieces.append(lower_raw - jnp.min(lower_raw))
        pieces.append(extent - (upper_raw - jnp.min(upper_raw)))
    return jnp.stack(pieces, axis=1).astype(jnp.int32)


def levels(own_key, shape, shards, low, high):
    def one(dim, shards_of):
        steps = jax.random.uniform(jax.random.fold_in(jax.random.fold_in(own_key, 6), dim), (shards_of,), jnp.float32, low / len(shards), high / len(shards))
        return jnp.repeat(jnp.exp(steps), shape[dim] // shards_of).reshape((-1,) + (1,) * (len(shape) - dim - 1))

    gain = one(*shards[0])
    for cut in shards[1:]:
        gain = gain * one(*cut)
    return gain


def centred(own_key, dims, deviation, reach, cuts=(), kind=jnp.bfloat16):
    loudness = levels(own_key, dims, cuts, -0.22, 0.18) if cuts else 1.0
    values = jax.random.normal(own_key, dims, jnp.float32) * deviation * loudness
    return jnp.minimum(jnp.maximum(values, -reach), reach).astype(kind)


def setup_inputs(seed: int = 0) -> dict:
    streams_of = jax.random.split(jax.random.key(seed), 11)
    return {
        "tokens": centred(streams_of[0], (CLIPS, FRAMES, PATCHES, D), 1.0, 6.0, ((0, 2), (2, 64))),
        "modulation": centred(streams_of[1], (CLIPS, 2, 2, 6, D), 0.6, 3.0, ((0, 2),), jnp.float32),
        "box_bounds": draw_box_bounds(jax.random.fold_in(streams_of[10], 71), 0),
        "masters": draw_masters(jax.random.fold_in(streams_of[10], 71), 0),
        "left_stats": draw_left_stats(jax.random.fold_in(streams_of[10], 71), 0),
        "right_stats": draw_right_stats(jax.random.fold_in(streams_of[10], 71), 0),
        "left_roots": draw_left_roots(jax.random.fold_in(streams_of[10], 71), 0),
        "right_roots": draw_right_roots(jax.random.fold_in(streams_of[10], 71), 0),
        "owner_slot": draw_owner_slot(jax.random.fold_in(streams_of[10], 71), 0),
        "cotangent": centred(streams_of[9], (CLIPS, FRAMES, PATCHES, D), 1.0, 6.0, ((0, 2), (2, 64))),
    }


@jax.custom_vjp
def low(v):
    return lax.optimization_barrier(v.astype(jnp.bfloat16)).astype(jnp.float32)

@jax.custom_vjp
def low_back(v):
    return v

def low_keep(v):
    return (low(v), None)

def low_pass(kept, grad):
    return (grad,)

def back_keep(v):
    return (v, None)

def back_low(kept, grad):
    return (low(grad),)
low.defvjp(low_keep, low_pass)
low_back.defvjp(back_keep, back_low)
highest = lax.Precision.HIGHEST
stat_decay = 0.5
learning_rate = 0.7
norm_epsilon = 1e-06

def layer_norm(values):
    center = values - lax.optimization_barrier(jnp.mean(values, axis=-1, keepdims=True))
    spread = lax.optimization_barrier(jnp.mean(center * center, axis=-1, keepdims=True))
    return center * lax.rsqrt(spread + norm_epsilon)

def inside(box_bounds, frame_ids, row_ids, col_ids):

    def edge_at(column):
        return box_bounds[:, column][:, None, None]
    return (edge_at(0) <= frame_ids) & (frame_ids < edge_at(1)) & (edge_at(2) <= row_ids) & (row_ids < edge_at(3)) & (edge_at(4) <= col_ids) & (col_ids < edge_at(5))

def assemble(tile_set):
    layers = []
    offset = 0
    for layer_index in range(2):
        matrices = []
        for row_count, col_count in ((D, 3 * D), (D, D), (D, FF), (FF, D)):
            tile_count = row_count // BLOCK * (col_count // BLOCK)
            tile_block = tile_set[offset:offset + tile_count].reshape(row_count // BLOCK, col_count // BLOCK, BLOCK, BLOCK)
            matrices.append(tile_block.transpose(0, 2, 1, 3).reshape(row_count, col_count))
            offset = offset + tile_count
        layers.append(matrices)
    return layers

def attention(normed, qkv_weight, spatial):
    frame_count, patch_count = (normed.shape[0], normed.shape[1])
    joined = jnp.dot(normed, qkv_weight, precision=highest)

    def split_heads(col_start):
        picked = low_back(low(joined[..., col_start:col_start + D]))
        return picked.reshape(frame_count, patch_count, HEADS, HD)
    queries, keyset, valueset = (split_heads(0), split_heads(D), split_heads(2 * D))
    if spatial:
        score_form, value_form = ('fqhe,fkhe->fhqk', 'fhqk,fkhe->fqhe')
    else:
        score_form, value_form = ('qphe,kphe->phqk', 'phqk,kphe->qphe')
    scores = low_back(jnp.einsum(score_form, queries, keyset, precision=highest) * HD ** (-0.5))
    probs_low = low(jax.nn.softmax(scores, axis=-1))
    attended = jnp.einsum(value_form, probs_low, valueset, precision=highest)
    return low_back(low(attended)).reshape(frame_count, patch_count, D)

def block(residual, modulate, in_box, weights, spatial):
    qkv_weight, out_weight, first_weight, second_weight = weights
    picked = jnp.where(in_box[..., None, None], modulate[1], modulate[0])
    normed = low(layer_norm(residual) * (1.0 + picked[..., 1, :]) + picked[..., 0, :])
    branch = low_back(jnp.dot(attention(normed, qkv_weight, spatial), out_weight, precision=highest))
    middle = residual + picked[..., 2, :] * branch
    renormed = low(layer_norm(middle) * (1.0 + picked[..., 4, :]) + picked[..., 3, :])
    hidden = low_back(jnp.dot(renormed, first_weight, precision=highest))
    active = low(jax.nn.gelu(hidden))
    mlp_out = low_back(jnp.dot(active, second_weight, precision=highest))
    return middle + picked[..., 5, :] * mlp_out

def reference(tokens, modulation, box_bounds, masters, left_stats, right_stats, left_roots, right_roots, owner_slot, cotangent):
    frame_ids = jnp.arange(FRAMES, dtype=jnp.int32)[None, :, None]
    patch_ids = jnp.arange(PATCHES, dtype=jnp.int32)[None, None, :]
    in_boxes = inside(box_bounds, frame_ids, patch_ids // GRID, patch_ids % GRID)

    def forward(residual_all, master_slots):
        layers = assemble(low(master_slots)[owner_slot])

        def one_clip(packed):
            residual, modulate, in_box = packed
            middle = block(residual, modulate[0], in_box, layers[0], True)
            return block(middle, modulate[1], in_box, layers[1], False)
        return lax.map(jax.checkpoint(one_clip), (residual_all, modulation, in_boxes))
    outputs, pullback = jax.vjp(forward, tokens.astype(jnp.float32), masters)
    token_grads, tile_grads = pullback(cotangent.astype(jnp.float32))
    product_left = jnp.einsum('sij,skj->sik', tile_grads, tile_grads, precision=highest)
    product_right = jnp.einsum('sji,sjk->sik', tile_grads, tile_grads, precision=highest)
    new_left = stat_decay * left_stats + (1.0 - stat_decay) * product_left
    new_right = stat_decay * right_stats + (1.0 - stat_decay) * product_right
    rotated = jnp.einsum('sij,sjk->sik', tile_grads, right_roots, precision=highest)
    update = jnp.einsum('sij,sjk->sik', left_roots, rotated, precision=highest)
    new_masters = masters - learning_rate * update
    return (outputs.astype(jnp.bfloat16), token_grads.astype(jnp.bfloat16), tile_grads, new_left, new_right, new_masters)
```

```python
import functools

import jax
import jax.numpy as jnp
from jax import lax
from jax.experimental import pallas as pl
from jax.experimental.pallas import tpu as pltpu
from jax.sharding import Mesh
from jax.sharding import PartitionSpec as P

D = 768
HEADS = 12
HD = 64
FF = 3072
GRID = 16
BLOCK = 128
TOK = 256
CH = 256
POS = ("pos_0", "pos_1", "pos_2", "pos_3")
EVERY = ("pos_0", "pos_1", "pos_2", "pos_3", "frame")

highest = lax.Precision.HIGHEST
stat_decay = 0.5
learning_rate = 0.7
norm_epsilon = 1e-06
f32 = jnp.float32
bf16 = jnp.bfloat16

QKV_AT, OUT_AT, FIRST_AT, SECOND_AT, LAYER_TILES = 0, 108, 144, 288, 432


def dot_nn(a, b):
    return lax.dot_general(a, b, (((1,), (0,)), ((), ())), preferred_element_type=f32)


def dot_nt(a, b):
    return lax.dot_general(a, b, (((1,), (1,)), ((), ())), preferred_element_type=f32)


def dot_tn(a, b):
    return lax.dot_general(a, b, (((0,), (0,)), ((), ())), preferred_element_type=f32)


def side(parts):
    return jnp.concatenate(parts, axis=1)


def norm_parts(values):
    center = values - jnp.mean(values, axis=-1, keepdims=True)
    spread = jnp.mean(center * center, axis=-1, keepdims=True)
    inverse = lax.rsqrt(spread + norm_epsilon)
    return center * inverse, inverse


def norm_back(normal, inverse, grad):
    return inverse * (
        grad
        - jnp.mean(grad, axis=-1, keepdims=True)
        - normal * jnp.mean(grad * normal, axis=-1, keepdims=True)
    )


def picked_row(mod_ref, mask_ref, row):
    clips = mod_ref.shape[0]
    span = TOK // clips
    parts = []
    for clip in range(clips):
        inside_box = jnp.broadcast_to(mask_ref[clip * span : (clip + 1) * span, :], (span, D)) > 0.5
        parts.append(
            jnp.where(
                inside_box,
                jnp.broadcast_to(mod_ref[clip, 1, row : row + 1, :], (span, D)),
                jnp.broadcast_to(mod_ref[clip, 0, row : row + 1, :], (span, D)),
            )
        )
    return parts[0] if clips == 1 else jnp.concatenate(parts, axis=0)


def fetch(slots_ref, owner_ref, held, sem, base, row_tiles, col_tiles):
    step = 6

    def one(turn, carry):
        col = turn // (row_tiles // step)
        first = (turn % (row_tiles // step)) * step
        for k in range(step):
            row = first + k
            pltpu.make_async_copy(
                slots_ref.at[owner_ref[base + row * col_tiles + col]],
                held.at[col, pl.ds(pl.multiple_of(row * BLOCK, BLOCK), BLOCK), :],
                sem,
            ).start()
        return carry

    lax.fori_loop(0, col_tiles * (row_tiles // step), one, 0)


def fetch_done(held, sem):
    pltpu.make_async_copy(held, held, sem).wait()


def forward_part(x, mod_ref, mask_ref, weights, waits, kept, same):
    wq, wo, w1, w2 = weights
    qkv_s, probs_s, attended_s, slope_s, active_s = kept
    lane = lax.broadcasted_iota(jnp.int32, (TOK, BLOCK), 1)
    low_half = lane < HD

    normal, _ = norm_parts(x)
    normed = (normal * (1.0 + picked_row(mod_ref, mask_ref, 1)) + picked_row(mod_ref, mask_ref, 0)).astype(bf16)
    waits[0]()

    def project(j, carry):
        qkv_s[j] = dot_nn(normed, side([wq[2 * j], wq[2 * j + 1]])).astype(bf16)
        return carry

    lax.fori_loop(0, 9, project, 0)

    def attend(c, carry):
        for pair in range(2):
            cols = slice(pair * BLOCK, (pair + 1) * BLOCK)
            q, k, v = qkv_s[c, :, cols], qkv_s[3 + c, :, cols], qkv_s[6 + c, :, cols]
            outs = []
            for e in range(2):
                mine = low_half if e == 0 else jnp.logical_not(low_half)
                scores = dot_nt(k, jnp.where(mine, q, jnp.zeros_like(q))) * HD ** (-0.5)
                if same is not None:
                    scores = jnp.where(same, scores, -jnp.inf)
                grown = jnp.exp(scores - jnp.max(scores, axis=0, keepdims=True))
                probs = (grown * (1.0 / jnp.sum(grown, axis=0, keepdims=True))).astype(bf16)
                probs_s[4 * c + 2 * pair + e] = probs
                outs.append(dot_tn(probs, v))
            attended_s[c, :, cols] = jnp.where(low_half, outs[0], outs[1]).astype(bf16)
        return carry

    lax.fori_loop(0, 3, attend, 0)
    attended = side([attended_s[c] for c in range(3)])
    waits[1]()
    branch = side([dot_nn(attended, side([wo[2 * j], wo[2 * j + 1]])) for j in range(3)])
    middle = x + picked_row(mod_ref, mask_ref, 2) * branch
    normal, _ = norm_parts(middle)
    renormed = (normal * (1.0 + picked_row(mod_ref, mask_ref, 4)) + picked_row(mod_ref, mask_ref, 3)).astype(bf16)
    waits[2]()

    def widen(j, carry):
        u = dot_nn(renormed, side([w1[2 * j], w1[2 * j + 1]]))
        root = (2.0 / 3.141592653589793) ** 0.5
        square = u * u
        bent = jnp.tanh(root * (u + 0.044715 * (square * u)))
        active_s[j] = (0.5 * u * (1.0 + bent)).astype(bf16)
        slope_s[j] = (
            0.5 * (1.0 + bent) + 0.5 * u * (1.0 - bent * bent) * (root * (1.0 + 3 * 0.044715 * square))
        ).astype(bf16)
        return carry

    lax.fori_loop(0, 12, widen, 0)
    active = side([active_s[j] for j in range(12)])
    waits[3]()
    mlp = side([dot_nn(active, side([w2[2 * j], w2[2 * j + 1]])) for j in range(3)])
    return middle, renormed, middle + picked_row(mod_ref, mask_ref, 5) * mlp


def send_tiles(stage, grads_ref, place_ref, sem, at, col_tiles, value, row, col):
    rows, cols = value.shape[0] // BLOCK, value.shape[1] // BLOCK
    for j in range(cols):
        for i in range(rows):
            tile = at + (row + i) * col_tiles + (col + j)
            stage[tile] = value[i * BLOCK : (i + 1) * BLOCK, j * BLOCK : (j + 1) * BLOCK].astype(bf16)
            pltpu.make_async_copy(stage.at[tile], grads_ref.at[place_ref[tile]], sem).start()


def backward_part(x, middle, renormed, upstream, mod_ref, mask_ref, weights, waits, kept, stage, grads_ref, place_ref, sem, acc, wide_s):
    wq, wo, w1, w2 = weights
    qkv_s, probs_s, attended_s, slope_s, active_s = kept
    lane = lax.broadcasted_iota(jnp.int32, (TOK, BLOCK), 1)
    low_half = lane < HD
    send = functools.partial(send_tiles, stage, grads_ref, place_ref, sem)

    grad_mlp = (picked_row(mod_ref, mask_ref, 5) * upstream).astype(bf16)
    renormed_t = renormed.T
    acc[...] = jnp.zeros_like(acc)
    waits[3]()
    waits[2]()

    def narrow(j, carry):
        rows = pl.ds(pl.multiple_of(j * CH, CH), CH)
        grad_active = dot_nt(grad_mlp, side([w2[n, rows, :] for n in range(6)]))
        grad_hidden = (grad_active * slope_s[j].astype(f32)).astype(bf16)
        acc[...] += dot_nt(grad_hidden, side([w1[2 * j], w1[2 * j + 1]]))
        send(FIRST_AT, 24, dot_nn(renormed_t, grad_hidden), 0, 2 * j)
        send(SECOND_AT, 6, dot_tn(active_s[j], grad_mlp), 2 * j, 0)
        return carry

    lax.fori_loop(0, 12, narrow, 0)
    normal, inverse = norm_parts(middle)
    grad_middle = upstream + norm_back(normal, inverse, (1.0 + picked_row(mod_ref, mask_ref, 4)) * acc[...])
    grad_branch = (picked_row(mod_ref, mask_ref, 2) * grad_middle).astype(bf16)
    waits[1]()

    def attend(c, carry):
        rows = pl.ds(pl.multiple_of(c * CH, CH), CH)
        grad_attended = dot_nt(grad_branch, side([wo[n, rows, :] for n in range(6)])).astype(bf16)
        send(OUT_AT, 6, dot_tn(attended_s[c], grad_branch), 2 * c, 0)
        for pair in range(2):
            cols = slice(pair * BLOCK, (pair + 1) * BLOCK)
            q, k, v = qkv_s[c, :, cols], qkv_s[3 + c, :, cols], qkv_s[6 + c, :, cols]
            ga = grad_attended[:, cols]
            grads = []
            for e in range(2):
                mine = low_half if e == 0 else jnp.logical_not(low_half)
                probs_low = probs_s[4 * c + 2 * pair + e]
                probs = probs_low.astype(f32)
                weighed = probs * dot_nt(v, jnp.where(mine, ga, jnp.zeros_like(ga)))
                grad_scores = (weighed - probs * jnp.sum(weighed, axis=0, keepdims=True)).astype(bf16)
                grads.append((dot_tn(grad_scores, k), dot_nn(grad_scores, q), dot_nn(probs_low, ga)))
            for n, scaling in ((0, HD ** (-0.5)), (1, HD ** (-0.5)), (2, 1.0)):
                wide_s[3 * n + c, :, cols] = (
                    jnp.where(low_half, grads[0][n], grads[1][n]) * scaling
                ).astype(bf16)
        return carry

    lax.fori_loop(0, 3, attend, 0)
    normal, inverse = norm_parts(x)
    scale_one = 1.0 + picked_row(mod_ref, mask_ref, 1)
    normed_t = (normal * scale_one + picked_row(mod_ref, mask_ref, 0)).astype(bf16).T
    acc[...] = jnp.zeros_like(acc)
    waits[0]()

    def gather_in(j, carry):
        piece = wide_s[j]
        acc[...] += dot_nt(piece, side([wq[2 * j], wq[2 * j + 1]]))
        send(QKV_AT, 18, dot_nn(normed_t, piece), 0, 2 * j)
        return carry

    lax.fori_loop(0, 9, gather_in, 0)
    normal, inverse = norm_parts(x)
    return grad_middle + norm_back(normal, inverse, scale_one * acc[...])


def same_sequence():
    rows = lax.broadcasted_iota(jnp.int32, (TOK, TOK), 0)
    cols = lax.broadcasted_iota(jnp.int32, (TOK, TOK), 1)
    return jnp.logical_and(rows // 64 == cols // 64, rows % 4 == cols % 4)


WEIGHT_SCRATCH = [
    pltpu.VMEM((18, D, BLOCK), bf16),
    pltpu.VMEM((6, D, BLOCK), bf16),
    pltpu.VMEM((24, D, BLOCK), bf16),
    pltpu.VMEM((6, FF, BLOCK), bf16),
    pltpu.SemaphoreType.DMA((4,)),
]
KEPT = [
    ((9, TOK, CH), bf16),
    ((HEADS, TOK, TOK), bf16),
    ((3, TOK, CH), bf16),
    ((12, TOK, CH), bf16),
    ((12, TOK, CH), bf16),
]
WEIGHT_RUNS = ((QKV_AT, 6, 18), (OUT_AT, 6, 6), (FIRST_AT, 6, 24), (SECOND_AT, 24, 6))


def fetch_all(slots_ref, owner_ref, held, sems, base, order):
    for n in order:
        at, rows, cols = WEIGHT_RUNS[n]
        fetch(slots_ref, owner_ref, held[n], sems.at[n], base + at, rows, cols)
    return [functools.partial(fetch_done, held[n], sems.at[n]) for n in range(4)]


def first_forward(owner_ref, x_ref, mod_ref, mask_ref, slots_ref, middle_ref, out_ref, *rest):
    kept, (wq, wo, w1, w2, sems) = rest[:5], rest[5:]
    weights = (wq, wo, w1, w2)
    waits = fetch_all(slots_ref, owner_ref, weights, sems, 0, (0, 1, 2, 3))
    middle, _, output = forward_part(x_ref[...].astype(f32), mod_ref, mask_ref, weights, waits, kept, None)
    middle_ref[...] = middle
    out_ref[...] = output.astype(bf16)


def second_layer(
    owner_ref, place_ref, x_ref, up_ref, mod_ref, mask_ref, slots_ref, out_ref, grad_ref, grads_ref, *rest
):
    kept, (wq, wo, w1, w2, sems, stage, sem, acc, wide_s) = rest[:5], rest[5:]
    weights = (wq, wo, w1, w2)
    waits = fetch_all(slots_ref, owner_ref, weights, sems, LAYER_TILES, (0, 1, 2, 3))
    x = x_ref[...].astype(f32)
    middle, renormed, output = forward_part(x, mod_ref, mask_ref, weights, waits, kept, same_sequence())
    out_ref[...] = output.astype(bf16)
    nothing = [lambda: None] * 4
    grad = backward_part(
        x, middle, renormed, up_ref[...].astype(f32), mod_ref, mask_ref, weights, nothing, kept,
        stage, grads_ref, place_ref.at[pl.ds(LAYER_TILES, LAYER_TILES)], sem, acc, wide_s,
    )
    grad_ref[...] = grad.astype(bf16)
    pltpu.make_async_copy(stage, grads_ref.at[pl.ds(0, LAYER_TILES)], sem).wait()


def first_backward(
    owner_ref, place_ref, empty_ref, x_ref, middle_ref, up_ref, mod_ref, mask_ref, slots_ref,
    qkv_s, probs_s, attended_s, slope_s, active_s, _, grad_ref, grads_ref,
    wq, wo, w1, w2, sems, stage, sem, acc, wide_s, blank,
):
    weights = (wq, wo, w1, w2)
    waits = fetch_all(slots_ref, owner_ref, weights, sems, 0, (3, 2, 1, 0))
    blank[...] = jnp.zeros_like(blank)
    for k in range(32):
        pltpu.make_async_copy(blank.at[k], grads_ref.at[empty_ref[k]], sem).start()
    x, middle = x_ref[...].astype(f32), middle_ref[...]
    normal, _inverse = norm_parts(middle)
    renormed = (normal * (1.0 + picked_row(mod_ref, mask_ref, 4)) + picked_row(mod_ref, mask_ref, 3)).astype(bf16)
    grad = backward_part(
        x, middle, renormed, up_ref[...].astype(f32), mod_ref, mask_ref, weights, waits,
        (qkv_s, probs_s, attended_s, slope_s, active_s), stage, grads_ref, place_ref, sem, acc, wide_s,
    )
    grad_ref[...] = grad.astype(bf16)
    pltpu.make_async_copy(stage, grads_ref.at[pl.ds(0, LAYER_TILES)], sem).wait()
    pltpu.make_async_copy(blank, grads_ref.at[pl.ds(0, 32)], sem).wait()


SMEM = pl.BlockSpec(memory_space=pltpu.SMEM)
VMEM = pl.BlockSpec(memory_space=pltpu.VMEM)
ANY = pl.BlockSpec(memory_space=pl.ANY)
PARAMS = pltpu.CompilerParams(vmem_limit_bytes=60 * 1024 * 1024)
BACK_SCRATCH = [
    pltpu.VMEM((LAYER_TILES, BLOCK, BLOCK), bf16),
    pltpu.SemaphoreType.DMA,
    pltpu.VMEM((TOK, D), f32),
    pltpu.VMEM((9, TOK, CH), bf16),
]


def run_first_forward(owner, x, mod, mask, slots):
    return pl.pallas_call(
        first_forward,
        name="first_forward",
        out_shape=[jax.ShapeDtypeStruct((TOK, D), f32), jax.ShapeDtypeStruct((TOK, D), bf16)]
        + [jax.ShapeDtypeStruct(s, t) for s, t in KEPT],
        in_specs=[SMEM, VMEM, VMEM, VMEM, ANY],
        out_specs=[VMEM] * 7,
        scratch_shapes=WEIGHT_SCRATCH,
        compiler_params=PARAMS,
    )(owner, x, mod, mask, slots)


def run_second(owner, place, x, up, mod, mask, slots):
    return pl.pallas_call(
        second_layer,
        name="second_layer",
        out_shape=[
            jax.ShapeDtypeStruct((TOK, D), bf16),
            jax.ShapeDtypeStruct((TOK, D), bf16),
            jax.ShapeDtypeStruct(slots.shape, bf16),
        ],
        in_specs=[SMEM, SMEM, VMEM, VMEM, VMEM, VMEM, ANY],
        out_specs=[VMEM, VMEM, ANY],
        scratch_shapes=[pltpu.VMEM(s, t) for s, t in KEPT] + WEIGHT_SCRATCH + BACK_SCRATCH,
        compiler_params=PARAMS,
    )(owner, place, x, up, mod, mask, slots)


def run_first_backward(owner, place, empty, x, middle, up, mod, mask, slots, kept, grads):
    return pl.pallas_call(
        first_backward,
        name="first_backward",
        out_shape=[jax.ShapeDtypeStruct((TOK, D), bf16), jax.ShapeDtypeStruct(grads.shape, bf16)],
        in_specs=[SMEM] * 3 + [VMEM] * 5 + [ANY] + [VMEM] * 5 + [ANY],
        out_specs=[VMEM, ANY],
        scratch_shapes=WEIGHT_SCRATCH + BACK_SCRATCH + [pltpu.VMEM((32, BLOCK, BLOCK), bf16)],
        input_output_aliases={14: 1},
        compiler_params=PARAMS,
    )(owner, place, empty, x, middle, up, mod, mask, slots, *kept, grads)


def inside(box_bounds, frame_ids, patch_ids):
    row_ids, col_ids = patch_ids // GRID, patch_ids % GRID

    def edge(column):
        return box_bounds[..., column]

    return (
        (edge(0) <= frame_ids)
        & (frame_ids < edge(1))
        & (edge(2) <= row_ids)
        & (row_ids < edge(3))
        & (edge(4) <= col_ids)
        & (col_ids < edge(5))
    )


def everyone():
    for y in range(4):
        for xh in range(2):
            for z in range(4):
                for c in range(2):
                    for xl in range(2):
                        yield (y, xh, z, c, xl)


def number(y, xh, z, c, xl):
    return (((y * 2 + xh) * 4 + z) * 2 + c) * 2 + xl


def permute(value, target):
    return lax.ppermute(value, EVERY, [(number(*d), number(*target(*d))) for d in everyone()])


def along(axis, step):
    def target(y, xh, z, c, xl):
        if (axis == 0) == (c == 0):
            return ((y + step) % 4, xh, z, c, xl)
        return (y, xh, (z + step) % 4, c, xl)

    return target


def other_core(y, xh, z, c, xl):
    return (y, xh, z, 1 - c, xl)


def across(y, xh, z, c, xl):
    return (y, 1 - xh, z, c, 1 - xl)


def twin(y, xh, z, c, xl):
    return (y, xh, z, c, 1 - xl)


def added(*values):
    total = values[0].astype(f32)
    for value in values[1:]:
        total = total + value.astype(f32)
    return total.astype(bf16)


def ring_sum(blocks, axis, half):
    ahead = permute(blocks[2][:half], along(axis, 1))
    behind = permute(blocks[2][half:], along(axis, -1))
    up = jnp.concatenate([added(blocks[1][:half], ahead), blocks[1][half:]], axis=0)
    down = jnp.concatenate([blocks[3][:half], added(blocks[3][half:], behind)], axis=0)
    ahead = permute(up, along(axis, 1))
    behind = permute(down, along(axis, -1))
    return added(blocks[0], ahead, behind)


def reduce_tiles(grads, core):
    mine, others = grads[: 448], grads[448:]

    def joined(r):
        piece = slice(r * 112, (r + 1) * 112)
        return added(mine[piece], permute(others[piece], other_core))

    blocks = {r: joined(r) for r in (2, 1, 3, 0)}
    total = ring_sum(blocks, 0, 56)
    blocks = {r: total[r * 28 : (r + 1) * 28] for r in range(4)}
    total = ring_sum(blocks, 1, 14)
    part = added(total[:14], permute(total[14:], across))
    whole = part.astype(f32) + permute(part, twin).astype(f32)
    by_core = whole.reshape(2, 7, BLOCK, BLOCK)
    own = lax.dynamic_index_in_dim(by_core, core, 0, keepdims=False)
    given = lax.dynamic_index_in_dim(by_core, 1 - core, 0, keepdims=False)
    got = permute(given, other_core)
    return jnp.where(core == 0, jnp.concatenate([own, got], axis=0), jnp.concatenate([got, own], axis=0))


def place_of(slots, y, xh, z, core):
    owner, k = slots // 14, slots % 14
    owner_y, owner_xh, owner_z, owner_c = owner // 16, owner // 8 % 2, owner // 2 % 4, owner % 2
    handler = k // 7
    ahead_y, ahead_z = (owner_y - y) % 4, (owner_z - z) % 4
    first = jnp.where(handler == 0, ahead_y, ahead_z)
    second = jnp.where(handler == 0, ahead_z, ahead_y)
    place = (handler + core) % 2
    for extent, index in ((4, first), (4, second), (2, (owner_xh + xh) % 2), (2, owner_c), (7, k % 7)):
        place = place * extent + index
    return place.astype(jnp.int32)


def local(
    tokens,
    modulation,
    box_bounds,
    masters,
    left_stats,
    right_stats,
    left_roots,
    right_roots,
    owner_slot,
    cotangent,
):
    y, xh, z, core = (lax.axis_index(a) for a in POS)
    mine = lax.axis_index(POS)
    slots_all = lax.all_gather(masters.astype(bf16), POS, axis=0, tiled=True)

    def to_frames(value):
        return lax.all_to_all(value.reshape(64, 4, D), POS, 0, 0, tiled=True).reshape(TOK, D)

    clip, frame = mine // 16, mine % 16
    tokens_here = to_frames(tokens)
    mod_first = lax.dynamic_slice_in_dim(modulation[:, 0], clip, 1, 0)
    bounds_here = lax.dynamic_index_in_dim(box_bounds, clip, 0, keepdims=True)
    mask_first = inside(bounds_here, frame, jnp.arange(TOK, dtype=jnp.int32))
    mask_first = mask_first.astype(f32).reshape(TOK, 1)
    ids = jnp.arange(TOK, dtype=jnp.int32)
    bounds_rows = jnp.repeat(box_bounds, 64, axis=0)
    mask_second = inside(bounds_rows, ids // 4 % 16, mine * 4 + ids % 4).astype(f32).reshape(TOK, 1)

    place = place_of(owner_slot, y, xh, z, core)
    free = jnp.ones((896,), jnp.int32).at[owner_slot].set(0)
    empty = place_of(jnp.nonzero(free, size=32)[0].astype(jnp.int32), y, xh, z, core)

    middle, passed, *kept = run_first_forward(owner_slot, tokens_here, mod_first, mask_first, slots_all)
    here = to_frames(passed)
    block_output, grad_here, grads = run_second(
        owner_slot, place, here, cotangent.reshape(TOK, D), modulation[:, 1], mask_second, slots_all
    )
    upstream = to_frames(grad_here)
    token_grads, grads = run_first_backward(
        owner_slot, place, empty, tokens_here, middle, upstream, mod_first, mask_first, slots_all, kept, grads
    )
    token_grads = to_frames(token_grads)
    owned_grads = reduce_tiles(grads, core)

    product_left = jnp.einsum("sij,skj->sik", owned_grads, owned_grads, precision=highest)
    product_right = jnp.einsum("sji,sjk->sik", owned_grads, owned_grads, precision=highest)
    new_left = stat_decay * left_stats + (1.0 - stat_decay) * product_left
    new_right = stat_decay * right_stats + (1.0 - stat_decay) * product_right
    rotated = jnp.einsum("sij,sjk->sik", owned_grads, right_roots, precision=highest)
    update = jnp.einsum("sij,sjk->sik", left_roots, rotated, precision=highest)
    new_masters = masters - learning_rate * update
    return (
        block_output.reshape(tokens.shape),
        token_grads.reshape(tokens.shape),
        owned_grads,
        new_left,
        new_right,
        new_masters,
    )


def solution(mesh):
    split = Mesh(
        mesh.devices.reshape(4, 2, 4, 2, mesh.shape["frame"]),
        ("pos_0", "pos_1", "pos_2", "pos_3", "frame"),
    )
    return jax.shard_map(
        local,
        mesh=split,
        in_specs=(
            P("frame", None, POS, None),
            P("frame", None, None, None, None),
            P("frame", None),
            P(POS, None, None),
            P(POS, None, None),
            P(POS, None, None),
            P(POS, None, None),
            P(POS, None, None),
            P(),
            P("frame", None, POS, None),
        ),
        out_specs=(
            P("frame", None, POS, None),
            P("frame", None, POS, None),
            P(POS, None, None),
            P(POS, None, None),
            P(POS, None, None),
            P(POS, None, None),
        ),
        check_vma=False,
    )
```

```python
import functools

import jax
import jax.numpy as jnp
from jax import lax
from jax.experimental import pallas as pl
from jax.experimental.pallas import tpu as pltpu
from jax.sharding import Mesh
from jax.sharding import PartitionSpec as P

D = 768
HEADS = 12
HD = 64
FF = 3072
GRID = 16
BLOCK = 128
TOK = 256
CH = 256
POS = ("pos_0", "pos_1", "pos_2", "pos_3")
EVERY = ("pos_0", "pos_1", "pos_2", "pos_3", "frame")

highest = lax.Precision.HIGHEST
stat_decay = 0.5
learning_rate = 0.7
norm_epsilon = 1e-06
f32 = jnp.float32
bf16 = jnp.bfloat16

QKV_AT, OUT_AT, FIRST_AT, SECOND_AT, LAYER_TILES = 0, 108, 144, 288, 432


def dot_nn(a, b):
    return lax.dot_general(a, b, (((1,), (0,)), ((), ())), preferred_element_type=f32)


def dot_nt(a, b):
    return lax.dot_general(a, b, (((1,), (1,)), ((), ())), preferred_element_type=f32)


def dot_tn(a, b):
    return lax.dot_general(a, b, (((0,), (0,)), ((), ())), preferred_element_type=f32)


def side(parts):
    return jnp.concatenate(parts, axis=1)


def norm_parts(values):
    center = values - jnp.mean(values, axis=-1, keepdims=True)
    spread = jnp.mean(center * center, axis=-1, keepdims=True)
    inverse = lax.rsqrt(spread + norm_epsilon)
    return center * inverse, inverse


def norm_back(normal, inverse, grad):
    return inverse * (
        grad
        - jnp.mean(grad, axis=-1, keepdims=True)
        - normal * jnp.mean(grad * normal, axis=-1, keepdims=True)
    )


def picked_row(mod_ref, mask_ref, row):
    clips = mod_ref.shape[0]
    span = TOK // clips
    parts = []
    for clip in range(clips):
        inside_box = jnp.broadcast_to(mask_ref[clip * span : (clip + 1) * span, :], (span, D)) > 0.5
        parts.append(
            jnp.where(
                inside_box,
                jnp.broadcast_to(mod_ref[clip, 1, row : row + 1, :], (span, D)),
                jnp.broadcast_to(mod_ref[clip, 0, row : row + 1, :], (span, D)),
            )
        )
    return parts[0] if clips == 1 else jnp.concatenate(parts, axis=0)


def fetch(slots_ref, where_ref, held, sem, base, row_tiles, col_tiles):
    step = 6

    def one(turn, carry):
        col = turn // (row_tiles // step)
        first = (turn % (row_tiles // step)) * step
        for k in range(step):
            row = first + k
            target = held.at[col, pl.ds(pl.multiple_of(row * BLOCK, BLOCK), BLOCK), :]
            pltpu.make_async_copy(slots_ref.at[where_ref[base + row * col_tiles + col]], target, sem).start()
        return carry

    lax.fori_loop(0, col_tiles * (row_tiles // step), one, 0)


def fetch_done(held, sem):
    pltpu.make_async_copy(held, held, sem).wait()


def forward_part(x, mod_ref, mask_ref, weights, waits, kept, same):
    wq, wo, w1, w2 = weights
    qkv_s, probs_s, attended_s, slope_s, active_s = kept
    lane = lax.broadcasted_iota(jnp.int32, (TOK, BLOCK), 1)
    low_half = lane < HD

    normal, _ = norm_parts(x)
    normed = (normal * (1.0 + picked_row(mod_ref, mask_ref, 1)) + picked_row(mod_ref, mask_ref, 0)).astype(bf16)
    waits[0]()

    def project(j, carry):
        qkv_s[j] = dot_nn(normed, side([wq[2 * j], wq[2 * j + 1]])).astype(bf16)
        return carry

    lax.fori_loop(0, 9, project, 0)

    def attend(c, carry):
        for pair in range(2):
            cols = slice(pair * BLOCK, (pair + 1) * BLOCK)
            q, k, v = qkv_s[c, :, cols], qkv_s[3 + c, :, cols], qkv_s[6 + c, :, cols]
            outs = []
            for e in range(2):
                mine = low_half if e == 0 else jnp.logical_not(low_half)
                scores = dot_nt(k, jnp.where(mine, q, jnp.zeros_like(q))) * HD ** (-0.5)
                if same is not None:
                    scores = jnp.where(same, scores, -jnp.inf)
                grown = jnp.exp(scores - jnp.max(scores, axis=0, keepdims=True))
                probs = (grown * (1.0 / jnp.sum(grown, axis=0, keepdims=True))).astype(bf16)
                probs_s[4 * c + 2 * pair + e] = probs
                outs.append(dot_tn(probs, v))
            attended_s[c, :, cols] = jnp.where(low_half, outs[0], outs[1]).astype(bf16)
        return carry

    lax.fori_loop(0, 3, attend, 0)
    attended = side([attended_s[c] for c in range(3)])
    waits[1]()
    branch = side([dot_nn(attended, side([wo[2 * j], wo[2 * j + 1]])) for j in range(3)])
    middle = x + picked_row(mod_ref, mask_ref, 2) * branch
    normal, _ = norm_parts(middle)
    renormed = (normal * (1.0 + picked_row(mod_ref, mask_ref, 4)) + picked_row(mod_ref, mask_ref, 3)).astype(bf16)
    waits[2]()

    def widen(j, carry):
        u = dot_nn(renormed, side([w1[2 * j], w1[2 * j + 1]]))
        root = (2.0 / 3.141592653589793) ** 0.5
        square = u * u
        bent = jnp.tanh(root * (u + 0.044715 * (square * u)))
        active_s[j] = (0.5 * u * (1.0 + bent)).astype(bf16)
        slope_s[j] = (
            0.5 * (1.0 + bent) + 0.5 * u * (1.0 - bent * bent) * (root * (1.0 + 3 * 0.044715 * square))
        ).astype(bf16)
        return carry

    lax.fori_loop(0, 12, widen, 0)
    active = side([active_s[j] for j in range(12)])
    waits[3]()
    mlp = side([dot_nn(active, side([w2[2 * j], w2[2 * j + 1]])) for j in range(3)])
    return middle, renormed, middle + picked_row(mod_ref, mask_ref, 5) * mlp


def send_tile(tile_ref, place, grads_refs, sem):
    start = 0
    for ref in grads_refs:
        size = ref.shape[0]

        @pl.when(jnp.logical_and(place >= start, place < start + size))
        def _(ref=ref, start=start):
            pltpu.make_async_copy(tile_ref, ref.at[place - start], sem).start()

        start += size


def send_tiles(stage, grads_refs, place_ref, sem, at, col_tiles, value, row, col):
    rows, cols = value.shape[0] // BLOCK, value.shape[1] // BLOCK
    for j in range(cols):
        for i in range(rows):
            tile = at + (row + i) * col_tiles + (col + j)
            stage[tile] = value[i * BLOCK : (i + 1) * BLOCK, j * BLOCK : (j + 1) * BLOCK].astype(bf16)
            send_tile(stage.at[tile], place_ref[tile], grads_refs, sem)


def backward_part(x, middle, renormed, upstream, mod_ref, mask_ref, weights, waits, kept, stage, grads_refs, place_ref, sem, acc, wide_s):
    wq, wo, w1, w2 = weights
    qkv_s, probs_s, attended_s, slope_s, active_s = kept
    lane = lax.broadcasted_iota(jnp.int32, (TOK, BLOCK), 1)
    low_half = lane < HD
    send = functools.partial(send_tiles, stage, grads_refs, place_ref, sem)

    grad_mlp = (picked_row(mod_ref, mask_ref, 5) * upstream).astype(bf16)
    renormed_t = renormed.T
    acc[...] = jnp.zeros_like(acc)
    waits[3]()
    waits[2]()

    def narrow(j, carry):
        rows = pl.ds(pl.multiple_of(j * CH, CH), CH)
        grad_active = dot_nt(grad_mlp, side([w2[n, rows, :] for n in range(6)]))
        grad_hidden = (grad_active * slope_s[j].astype(f32)).astype(bf16)
        acc[...] += dot_nt(grad_hidden, side([w1[2 * j], w1[2 * j + 1]]))
        send(FIRST_AT, 24, dot_nn(renormed_t, grad_hidden), 0, 2 * j)
        send(SECOND_AT, 6, dot_tn(active_s[j], grad_mlp), 2 * j, 0)
        return carry

    lax.fori_loop(0, 12, narrow, 0)
    normal, inverse = norm_parts(middle)
    grad_middle = upstream + norm_back(normal, inverse, (1.0 + picked_row(mod_ref, mask_ref, 4)) * acc[...])
    grad_branch = (picked_row(mod_ref, mask_ref, 2) * grad_middle).astype(bf16)
    waits[1]()

    def attend(c, carry):
        rows = pl.ds(pl.multiple_of(c * CH, CH), CH)
        grad_attended = dot_nt(grad_branch, side([wo[n, rows, :] for n in range(6)])).astype(bf16)
        send(OUT_AT, 6, dot_tn(attended_s[c], grad_branch), 2 * c, 0)
        for pair in range(2):
            cols = slice(pair * BLOCK, (pair + 1) * BLOCK)
            q, k, v = qkv_s[c, :, cols], qkv_s[3 + c, :, cols], qkv_s[6 + c, :, cols]
            ga = grad_attended[:, cols]
            grads = []
            for e in range(2):
                mine = low_half if e == 0 else jnp.logical_not(low_half)
                probs_low = probs_s[4 * c + 2 * pair + e]
                probs = probs_low.astype(f32)
                weighed = probs * dot_nt(v, jnp.where(mine, ga, jnp.zeros_like(ga)))
                grad_scores = (weighed - probs * jnp.sum(weighed, axis=0, keepdims=True)).astype(bf16)
                grads.append((dot_tn(grad_scores, k), dot_nn(grad_scores, q), dot_nn(probs_low, ga)))
            for n, scaling in ((0, HD ** (-0.5)), (1, HD ** (-0.5)), (2, 1.0)):
                wide_s[3 * n + c, :, cols] = (
                    jnp.where(low_half, grads[0][n], grads[1][n]) * scaling
                ).astype(bf16)
        return carry

    lax.fori_loop(0, 3, attend, 0)
    normal, inverse = norm_parts(x)
    scale_one = 1.0 + picked_row(mod_ref, mask_ref, 1)
    normed_t = (normal * scale_one + picked_row(mod_ref, mask_ref, 0)).astype(bf16).T
    acc[...] = jnp.zeros_like(acc)
    waits[0]()

    def gather_in(j, carry):
        piece = wide_s[j]
        acc[...] += dot_nt(piece, side([wq[2 * j], wq[2 * j + 1]]))
        send(QKV_AT, 18, dot_nn(normed_t, piece), 0, 2 * j)
        return carry

    lax.fori_loop(0, 9, gather_in, 0)
    normal, inverse = norm_parts(x)
    return grad_middle + norm_back(normal, inverse, scale_one * acc[...])


def same_sequence():
    rows = lax.broadcasted_iota(jnp.int32, (TOK, TOK), 0)
    cols = lax.broadcasted_iota(jnp.int32, (TOK, TOK), 1)
    return jnp.logical_and(rows // 64 == cols // 64, rows % 4 == cols % 4)


WEIGHT_SCRATCH = [
    pltpu.VMEM((18, D, BLOCK), bf16),
    pltpu.VMEM((6, D, BLOCK), bf16),
    pltpu.VMEM((24, D, BLOCK), bf16),
    pltpu.VMEM((6, FF, BLOCK), bf16),
    pltpu.SemaphoreType.DMA((4,)),
]
KEPT = [
    ((9, TOK, CH), bf16),
    ((HEADS, TOK, TOK), bf16),
    ((3, TOK, CH), bf16),
    ((12, TOK, CH), bf16),
    ((12, TOK, CH), bf16),
]
WEIGHT_RUNS = ((QKV_AT, 6, 18), (OUT_AT, 6, 6), (FIRST_AT, 6, 24), (SECOND_AT, 24, 6))


def fetch_all(slots_ref, where_ref, held, sems, base, order):
    for n in order:
        at, rows, cols = WEIGHT_RUNS[n]
        fetch(slots_ref, where_ref, held[n], sems.at[n], base + at, rows, cols)
    return [functools.partial(fetch_done, held[n], sems.at[n]) for n in range(4)]


def first_forward(where_ref, x_ref, mod_ref, mask_ref, slots_ref, middle_ref, out_ref, *rest):
    kept, (wq, wo, w1, w2, sems) = rest[:5], rest[5:]
    weights = (wq, wo, w1, w2)
    waits = fetch_all(slots_ref, where_ref, weights, sems, 0, (0, 1, 2, 3))
    middle, _, output = forward_part(x_ref[...].astype(f32), mod_ref, mask_ref, weights, waits, kept, None)
    middle_ref[...] = middle
    out_ref[...] = output.astype(bf16)


def second_layer(
    where_ref, place_ref, x_ref, up_ref, mod_ref, mask_ref, slots_ref, out_ref, grad_ref, *rest
):
    grads_refs, rest = rest[:6], rest[6:]
    kept, (wq, wo, w1, w2, sems, stage, sem, acc, wide_s) = rest[:5], rest[5:]
    weights = (wq, wo, w1, w2)
    waits = fetch_all(slots_ref, where_ref, weights, sems, LAYER_TILES, (0, 1, 2, 3))
    x = x_ref[...].astype(f32)
    middle, renormed, output = forward_part(x, mod_ref, mask_ref, weights, waits, kept, same_sequence())
    out_ref[...] = output.astype(bf16)
    nothing = [lambda: None] * 4
    grad = backward_part(
        x, middle, renormed, up_ref[...].astype(f32), mod_ref, mask_ref, weights, nothing, kept,
        stage, grads_refs, place_ref.at[pl.ds(LAYER_TILES, LAYER_TILES)], sem, acc, wide_s,
    )
    grad_ref[...] = grad.astype(bf16)
    pltpu.make_async_copy(stage, stage, sem).wait()


def first_backward(
    where_ref, place_ref, empty_ref, x_ref, middle_ref, up_ref, mod_ref, mask_ref, slots_ref,
    qkv_s, probs_s, attended_s, slope_s, active_s, *rest,
):
    grad_ref, *grads_refs = rest[6:13]
    wq, wo, w1, w2, sems, stage, sem, acc, wide_s, blank = rest[13:]
    weights = (wq, wo, w1, w2)
    waits = fetch_all(slots_ref, where_ref, weights, sems, 0, (3, 2, 1, 0))
    blank[...] = jnp.zeros_like(blank)
    for k in range(32):
        send_tile(blank.at[k], empty_ref[k], grads_refs, sem)
    x, middle = x_ref[...].astype(f32), middle_ref[...]
    normal, _inverse = norm_parts(middle)
    renormed = (normal * (1.0 + picked_row(mod_ref, mask_ref, 4)) + picked_row(mod_ref, mask_ref, 3)).astype(bf16)
    grad = backward_part(
        x, middle, renormed, up_ref[...].astype(f32), mod_ref, mask_ref, weights, waits,
        (qkv_s, probs_s, attended_s, slope_s, active_s), stage, grads_refs, place_ref, sem, acc, wide_s,
    )
    grad_ref[...] = grad.astype(bf16)
    pltpu.make_async_copy(stage, stage, sem).wait()
    pltpu.make_async_copy(blank, blank, sem).wait()


SMEM = pl.BlockSpec(memory_space=pltpu.SMEM)
VMEM = pl.BlockSpec(memory_space=pltpu.VMEM)
ANY = pl.BlockSpec(memory_space=pl.ANY)
PARAMS = pltpu.CompilerParams(vmem_limit_bytes=60 * 1024 * 1024)
BACK_SCRATCH = [
    pltpu.VMEM((LAYER_TILES, BLOCK, BLOCK), bf16),
    pltpu.SemaphoreType.DMA,
    pltpu.VMEM((TOK, D), f32),
    pltpu.VMEM((9, TOK, CH), bf16),
]


PARTS = (140, 112, 196)
GRADS = [jax.ShapeDtypeStruct((n, BLOCK, BLOCK), bf16) for n in PARTS + PARTS]


def run_first_forward(where, x, mod, mask, slots):
    return pl.pallas_call(
        first_forward,
        name="first_forward",
        out_shape=[jax.ShapeDtypeStruct((TOK, D), f32), jax.ShapeDtypeStruct((TOK, D), bf16)]
        + [jax.ShapeDtypeStruct(s, t) for s, t in KEPT],
        in_specs=[SMEM, VMEM, VMEM, VMEM] + [ANY],
        out_specs=[VMEM] * 7,
        scratch_shapes=WEIGHT_SCRATCH,
        compiler_params=PARAMS,
    )(where, x, mod, mask, slots)


def run_second(where, place, x, up, mod, mask, slots):
    return pl.pallas_call(
        second_layer,
        name="second_layer",
        out_shape=[
            jax.ShapeDtypeStruct((TOK, D), bf16),
            jax.ShapeDtypeStruct((TOK, D), bf16),
            *GRADS,
        ],
        in_specs=[SMEM, SMEM, VMEM, VMEM, VMEM, VMEM] + [ANY],
        out_specs=[VMEM, VMEM] + [ANY] * 6,
        scratch_shapes=[pltpu.VMEM(s, t) for s, t in KEPT] + WEIGHT_SCRATCH + BACK_SCRATCH,
        compiler_params=PARAMS,
    )(where, place, x, up, mod, mask, slots)


def run_first_backward(where, place, empty, x, middle, up, mod, mask, slots, kept, grads):
    return pl.pallas_call(
        first_backward,
        name="first_backward",
        out_shape=[
            jax.ShapeDtypeStruct((TOK, D), bf16),
            *GRADS,
        ],
        in_specs=[SMEM] * 3 + [VMEM] * 5 + [ANY] + [VMEM] * 5 + [ANY] * 6,
        out_specs=[VMEM] + [ANY] * 6,
        scratch_shapes=WEIGHT_SCRATCH + BACK_SCRATCH + [pltpu.VMEM((32, BLOCK, BLOCK), bf16)],
        input_output_aliases={14 + k: 1 + k for k in range(6)},
        compiler_params=PARAMS,
    )(where, place, empty, x, middle, up, mod, mask, slots, *kept, *grads)


def inside(box_bounds, frame_ids, patch_ids):
    row_ids, col_ids = patch_ids // GRID, patch_ids % GRID

    def edge(column):
        return box_bounds[..., column]

    return (
        (edge(0) <= frame_ids)
        & (frame_ids < edge(1))
        & (edge(2) <= row_ids)
        & (row_ids < edge(3))
        & (edge(4) <= col_ids)
        & (col_ids < edge(5))
    )


def everyone():
    for y in range(4):
        for xh in range(2):
            for z in range(4):
                for c in range(2):
                    for xl in range(2):
                        yield (y, xh, z, c, xl)


def number(y, xh, z, c, xl):
    return (((y * 2 + xh) * 4 + z) * 2 + c) * 2 + xl


def permute(value, target):
    return lax.ppermute(value, EVERY, [(number(*d), number(*target(*d))) for d in everyone()])


def along(axis, step):
    def target(y, xh, z, c, xl):
        if (axis == 0) == (c == 0):
            return ((y + step) % 4, xh, z, c, xl)
        return (y, xh, (z + step) % 4, c, xl)

    return target


def other_core(y, xh, z, c, xl):
    return (y, xh, z, 1 - c, xl)


def across(y, xh, z, c, xl):
    return (y, 1 - xh, z, c, 1 - xl)


def twin(y, xh, z, c, xl):
    return (y, xh, z, c, 1 - xl)


def added(*values):
    total = values[0].astype(f32)
    for value in values[1:]:
        total = total + value.astype(f32)
    return total.astype(bf16)


def pair(y, xh, z, c, xl):
    return twin(y, xh, z, c, xl) if c == 0 else across(y, xh, z, c, xl)


def opposite(y, xh, z, c, xl):
    return (y, 1 - xh, z, c, xl)


def pair_last(y, xh, z, c, xl):
    return across(y, xh, z, c, xl) if c == 0 else twin(y, xh, z, c, xl)


PIECES = {
    "plain2": (0, 56), "given2": (56, 28), "given13": (84, 56), "plain13": (140, 112), "kept2": (252, 28),
    "kept13": (280, 56), "given0": (336, 28), "kept0": (364, 28), "plain0": (392, 56),
}
TILE_STEP = 7


def add_tiles(plan, source_count, last_count, *refs):
    sources, outs = refs[:source_count], refs[source_count + last_count :]
    for out, parts in zip(outs, plan):
        for at, size, terms in parts:
            step = TILE_STEP if size % TILE_STEP == 0 else size

            def some(i, carry, out=out, at=at, terms=terms, step=step):
                for k in range(step):
                    n = i * step + k
                    total = sources[terms[0][0]][terms[0][1] + n].astype(f32)
                    for source, start in terms[1:]:
                        total = total + sources[source][start + n].astype(f32)
                    out[at + n] = total.astype(bf16)
                return carry

            lax.fori_loop(0, size // step, some, 0)


def keep(*refs):
    pass


FREE = pl.CostEstimate(flops=1, bytes_accessed=1, transcendentals=0)


class TileSums:
    def __init__(self):
        self.last = []

    def __call__(self, plan, *sources, after=None):
        sizes = [sum(size for _, size, _ in parts) for parts in plan]
        last = self.last if after is None else [*self.last, after]
        outs = pl.pallas_call(
            functools.partial(add_tiles, plan, len(sources), len(last)),
            name="add_tiles",
            out_shape=[jax.ShapeDtypeStruct((n, BLOCK, BLOCK), bf16) for n in sizes]
            + [jax.ShapeDtypeStruct((8, BLOCK), f32)],
            in_specs=[VMEM] * len(sources) + [ANY] * len(last),
            out_specs=[VMEM] * len(sizes) + [ANY],
            compiler_params=pltpu.CompilerParams(vmem_limit_bytes=16 * 1024 * 1024),
            cost_estimate=FREE,
        )(*sources, *last)
        self.last = [outs[-1]]
        return outs[:-1]

    def then(self, value):
        return pl.pallas_call(
            keep,
            name="keep",
            out_shape=jax.ShapeDtypeStruct(value.shape, value.dtype),
            in_specs=[ANY] * 2,
            out_specs=ANY,
            input_output_aliases={0: 0},
            cost_estimate=FREE,
        )(value, *self.last)


def reduce_tiles(mine, given, core, frame, token_blocks, send_tokens):
    add = TileSums()
    at = {name: start for name, (start, _) in PIECES.items()}

    def alone(size, *terms):
        return [(0, size, list(terms))]

    got = permute(given[0], other_core)
    p2_a, p2_b, over = add(
        [alone(28, (0, 0), (1, 0)), alone(28, (0, 28), (1, 28)), alone(84, (0, 56), (1, 56))], mine[0], got
    )
    p2_ahead, p2_behind = permute(p2_a, along(0, 1)), permute(p2_b, along(0, -1))
    x213 = permute(over, pair)
    got = permute(add.then(given[1]), other_core)
    last_got = permute(add.then(given[2]), other_core)
    p13 = add(
        [
            [(0, 28, [(0, 0), (1, 0), (2, 0)]), (28, 28, [(0, 28), (1, 28)])],
            [(0, 28, [(0, 56), (1, 56)]), (28, 28, [(0, 84), (1, 84), (3, 0)])],
        ],
        mine[1], got, p2_ahead, p2_behind,
    )
    p1, p3 = permute(p13[0], along(0, 1)), permute(p13[1], along(0, -1))
    mine, got = mine[2], last_got
    at = {name: start - 252 for name, start in at.items()}
    x0 = permute(add([alone(28, (0, at["given0"]), (1, at["given0"]))], mine, got)[0], pair)
    h2 = add([alone(14, (0, at["kept2"] + n), (1, at["kept2"] + n), (2, n)) for n in (0, 14)], mine, got, x213)
    h2_ahead, h2_behind = permute(h2[0], along(0, 1)), permute(h2[1], along(0, -1))

    def split(start, cuts):
        return [
            alone(size, (0, start + n), (1, start + n), *((k, n) for k in more)) for n, size, more in cuts
        ]

    p = add(
        split(at["plain0"], [(28, 7, (2, 3)), (35, 7, (2, 3)), (0, 14, (2, 3)), (14, 14, (2, 3)), (42, 14, (2, 3))]),
        mine, got, p1, p3,
    )
    ahead, behind = permute(p[0], along(1, 1)), permute(p[1], along(1, -1))
    k13 = r13 = at["kept13"]
    h13 = add(
        [
            [(0, 14, [(0, k13), (1, r13), (2, 28), (3, 0)]), (14, 14, [(0, k13 + 14), (1, r13 + 14), (2, 42)])],
            [(0, 14, [(0, k13 + 28), (1, r13 + 28), (2, 56)]), (14, 14, [(0, k13 + 42), (1, r13 + 42), (2, 70), (4, 0)])],
        ],
        mine, got, x213, h2_ahead, h2_behind,
    )
    h1, h3 = permute(h13[0], along(0, 1)), permute(h13[1], along(0, -1))
    sides = add(
        [
            [(0, 7, [(0, 0), (1, 0)]), (7, 7, [(0, 7)])],
            [(0, 7, [(2, 0)]), (7, 7, [(2, 7), (3, 0)])],
        ],
        p[3], ahead, p[4], behind,
    )
    up, down = permute(sides[0], along(1, 1)), permute(sides[1], along(1, -1))
    h = add(
        split(at["kept0"], [(14, 4, (2, 3, 4)), (18, 3, (2, 3, 4)), (0, 7, (2, 3, 4)), (7, 7, (2, 3, 4)), (21, 7, (2, 3, 4))]),
        mine, got, x0, h1, h3,
    )
    h_ahead, h_behind = permute(h[0], along(1, 1)), permute(h[1], along(1, -1))
    p = add([alone(7, (0, n), (1, n), (2, n)) for n in (0, 7)], p[2], up, down)
    far = permute(p[1], across)
    sides = add(
        [
            [(0, 4, [(0, 0), (1, 0)]), (4, 3, [(0, 4)])],
            [(0, 4, [(2, 0)]), (4, 3, [(2, 4), (3, 0)])],
        ],
        h[3], h_ahead, h[4], h_behind,
    )
    h_up, h_down = permute(sides[0], along(1, 1)), permute(sides[1], along(1, -1))
    (p,) = add([alone(7, (0, 0), (1, 0))], p[0], far)
    match = permute(p, twin)
    (h,) = add([alone(7, (0, 0), (1, 0), (2, 0))], h[2], h_up, h_down)
    token_blocks = send_tokens(add.then(token_blocks))
    beyond, beside, around = permute(h, pair_last), permute(h, twin), permute(h, opposite)
    own = p.astype(f32) + match.astype(f32)
    told = (core == 0) & (frame == 1)
    h = added(jnp.where(told, beside, h), jnp.where(told, around, beyond))
    got = permute(h, other_core).astype(f32)
    owned = jnp.where(core == 0, jnp.concatenate([own, got], axis=0), jnp.concatenate([got, own], axis=0))
    return owned, token_blocks


def pin(values, *after):
    return pl.pallas_call(
        keep,
        name="pin",
        out_shape=[jax.ShapeDtypeStruct(value.shape, value.dtype) for value in values],
        in_specs=[ANY] * (len(values) + len(after)),
        out_specs=[ANY] * len(values),
        input_output_aliases={k: k for k in range(len(values))},
        cost_estimate=FREE,
    )(*values, *after)


def gather_tiles(tiles, core, frame, beside):
    here = jnp.where(core == 0, tiles[:7], tiles[7:])
    there = permute(jnp.where(core == 0, tiles[7:], tiles[:7]), other_core)
    far = permute(jnp.concatenate([here, there], axis=0), across)
    kept = jnp.where((core == 0) & (frame == 1), far[7:], there)
    base = jnp.concatenate([here, far[:7], kept], axis=0)
    behind, ahead = permute(base, along(1, 1)), permute(base, along(1, -1))
    plain_far, halved_far = permute(behind[:14], along(1, 1)), permute(ahead[14:], along(1, -1))
    plain = jnp.concatenate([base[:14], behind[:14], ahead[:14], plain_far], axis=0)
    halved = jnp.concatenate([base[14:], behind[14:], ahead[14:], halved_far], axis=0)
    plain, halved = pin([plain, halved])
    h_behind, h_ahead = permute(halved, along(0, 1)), permute(halved, along(0, -1))
    h_over = permute(halved, pair)
    plain, sides = pin([plain, jnp.concatenate([h_behind, h_ahead], axis=0)])
    p_behind, p_ahead = permute(plain, along(0, 1)), permute(plain, along(0, -1))
    over = permute(sides, pair)
    far_low, far_high = permute(sides[:14], along(0, 1)), permute(sides[42:], along(0, -1))
    p_behind, p_ahead, *beside = pin([p_behind, p_ahead, *beside])
    p_low, p_high = permute(p_behind[:28], along(0, 1)), permute(p_ahead[28:], along(0, -1))
    h_far = jnp.concatenate([far_low, far_high], axis=0)
    parts = [plain, halved, h_over, p_behind, p_ahead, sides, over, p_low, p_high, h_far, permute(h_far, pair)]
    told = [
        permute(jnp.concatenate(run, axis=0), other_core) for run in (parts[:3], parts[3:6], parts[6:7], parts[7:])
    ]
    return jnp.concatenate([parts[0], parts[1], *parts[2:], *told], axis=0), beside


def source_of(slots, y, xh, z, core, frame):
    owner, k = slots // 14, slots % 14
    owner_y, owner_xh, owner_z, owner_c = owner // 16, owner // 8 % 2, owner // 2 % 4, owner % 2
    handler = k // 7
    ahead_y, ahead_z = (owner_y - y) % 4, (owner_z - z) % 4
    first = jnp.where(handler == 0, ahead_y, ahead_z)
    second = jnp.where(handler == 0, ahead_z, ahead_y)
    over_x = (owner_xh + xh) % 2
    kept = jnp.where(handler == 0, (over_x + frame) % 2, over_x) == 0
    rank = jnp.where(second == 3, 1, jnp.where(second == 1, 2, jnp.where(second == 2, 3, 0)))

    def start(own, behind, ahead, far):
        return jnp.where(first == 0, own, jnp.where(first == 3, behind, jnp.where(first == 1, ahead, far)))

    plain = start(0, 112, 168, 336) + rank * 14 + over_x * 7
    halved = jnp.where(kept, start(56, 224, 252, 392), start(84, 280, 308, 420)) + rank * 7
    place = jnp.where(owner_c == handler, plain, halved) + k % 7
    return ((handler + core) % 2 * 448 + place).astype(jnp.int32)


def place_of(slots, y, xh, z, core, frame):
    owner, k = slots // 14, slots % 14
    owner_y, owner_xh, owner_z, owner_c = owner // 16, owner // 8 % 2, owner // 2 % 4, owner % 2
    handler = k // 7
    ahead_y, ahead_z = (owner_y - y) % 4, (owner_z - z) % 4
    first = jnp.where(handler == 0, ahead_y, ahead_z)
    second = jnp.where(handler == 0, ahead_z, ahead_y)
    over_x = (owner_xh + xh) % 2
    kept = jnp.where(handler == 0, (over_x + frame) % 2, over_x) == 0

    def start(prefix, size):
        at0, at2, at13 = (PIECES[prefix + ring][0] for ring in ("0", "2", "13"))
        return jnp.where(first == 0, at0, jnp.where(first == 2, at2, at13 + size * (first // 2)))

    plain = start("plain", 56) + (second * 2 + over_x) * 7
    halved = jnp.where(kept, start("kept", 28), start("given", 28)) + second * 7
    place = jnp.where(owner_c == handler, plain, halved) + k % 7
    return ((handler + core) % 2 * 448 + place).astype(jnp.int32)


def local(
    tokens,
    modulation,
    box_bounds,
    masters,
    left_stats,
    right_stats,
    left_roots,
    right_roots,
    owner_slot,
    cotangent,
):
    y, xh, z, core = (lax.axis_index(a) for a in POS)
    mine, copy = lax.axis_index(POS), lax.axis_index("frame")

    def to_frames(value):
        return lax.all_to_all(value.reshape(64, 4, D), POS, 0, 0, tiled=True).reshape(TOK, D)

    clip, frame = mine // 16, mine % 16
    mod_first = lax.dynamic_slice_in_dim(modulation[:, 0], clip, 1, 0)
    bounds_here = lax.dynamic_index_in_dim(box_bounds, clip, 0, keepdims=True)
    mask_first = inside(bounds_here, frame, jnp.arange(TOK, dtype=jnp.int32))
    mask_first = mask_first.astype(f32).reshape(TOK, 1)
    ids = jnp.arange(TOK, dtype=jnp.int32)
    bounds_rows = jnp.repeat(box_bounds, 64, axis=0)
    mask_second = inside(bounds_rows, ids // 4 % 16, mine * 4 + ids % 4).astype(f32).reshape(TOK, 1)

    where = source_of(owner_slot, y, xh, z, core, copy)
    place = place_of(owner_slot, y, xh, z, core, copy)
    free = jnp.ones((896,), jnp.int32).at[owner_slot].set(0)
    empty = place_of(jnp.nonzero(free, size=32)[0].astype(jnp.int32), y, xh, z, core, copy)
    slots_all, (tokens_here, mod_first, mod_second, mask_first, mask_second, upstream, where, place, empty) = gather_tiles(
        masters.astype(bf16), core, copy,
        [
            to_frames(tokens), mod_first, modulation[:, 1], mask_first, mask_second,
            cotangent.reshape(TOK, D), where, place, empty,
        ],
    )

    middle, passed, *kept = run_first_forward(where, tokens_here, mod_first, mask_first, slots_all)
    here = to_frames(passed)
    block_output, grad_here, *grads = run_second(
        where, place, here, upstream, mod_second, mask_second, slots_all
    )
    upstream = to_frames(grad_here)
    token_grads, *grads = run_first_backward(
        where, place, empty, tokens_here, middle, upstream, mod_first, mask_first, slots_all, kept, grads
    )
    owned_grads, token_grads = reduce_tiles(grads[:3], grads[3:], core, copy, token_grads, to_frames)

    product_left = jnp.einsum("sij,skj->sik", owned_grads, owned_grads, precision=highest)
    product_right = jnp.einsum("sji,sjk->sik", owned_grads, owned_grads, precision=highest)
    new_left = stat_decay * left_stats + (1.0 - stat_decay) * product_left
    new_right = stat_decay * right_stats + (1.0 - stat_decay) * product_right
    rotated = jnp.einsum("sij,sjk->sik", owned_grads, right_roots, precision=highest)
    update = jnp.einsum("sij,sjk->sik", left_roots, rotated, precision=highest)
    new_masters = masters - learning_rate * update
    return (
        block_output.reshape(tokens.shape),
        token_grads.reshape(tokens.shape),
        owned_grads,
        new_left,
        new_right,
        new_masters,
    )


def solution(mesh):
    split = Mesh(
        mesh.devices.reshape(4, 2, 4, 2, mesh.shape["frame"]),
        ("pos_0", "pos_1", "pos_2", "pos_3", "frame"),
    )
    return jax.shard_map(
        local,
        mesh=split,
        in_specs=(
            P("frame", None, POS, None),
            P("frame", None, None, None, None),
            P("frame", None),
            P(POS, None, None),
            P(POS, None, None),
            P(POS, None, None),
            P(POS, None, None),
            P(POS, None, None),
            P(),
            P("frame", None, POS, None),
        ),
        out_specs=(
            P("frame", None, POS, None),
            P("frame", None, POS, None),
            P(POS, None, None),
            P(POS, None, None),
            P(POS, None, None),
            P(POS, None, None),
        ),
        check_vma=False,
    )
```

```python
import functools

import jax
import jax.numpy as jnp
from jax import lax
from jax.experimental import pallas as pl
from jax.experimental.pallas import tpu as pltpu
from jax.sharding import Mesh
from jax.sharding import PartitionSpec as P

D = 768
HEADS = 12
HD = 64
FF = 3072
GRID = 16
BLOCK = 128
TOK = 256
CH = 256
POS = ("pos_0", "pos_1", "pos_2", "pos_3")
EVERY = ("pos_0", "pos_1", "pos_2", "pos_3", "frame")

highest = lax.Precision.HIGHEST
stat_decay = 0.5
learning_rate = 0.7
norm_epsilon = 1e-06
f32 = jnp.float32
bf16 = jnp.bfloat16

QKV_AT, OUT_AT, FIRST_AT, SECOND_AT, LAYER_TILES = 0, 108, 144, 288, 432


def dot_nn(a, b):
    return lax.dot_general(a, b, (((1,), (0,)), ((), ())), preferred_element_type=f32)


def dot_nt(a, b):
    return lax.dot_general(a, b, (((1,), (1,)), ((), ())), preferred_element_type=f32)


def dot_tn(a, b):
    return lax.dot_general(a, b, (((0,), (0,)), ((), ())), preferred_element_type=f32)


def side(parts):
    return jnp.concatenate(parts, axis=1)


def norm_parts(values):
    center = values - jnp.mean(values, axis=-1, keepdims=True)
    spread = jnp.mean(center * center, axis=-1, keepdims=True)
    inverse = lax.rsqrt(spread + norm_epsilon)
    return center * inverse, inverse


def norm_back(normal, inverse, grad):
    return inverse * (
        grad
        - jnp.mean(grad, axis=-1, keepdims=True)
        - normal * jnp.mean(grad * normal, axis=-1, keepdims=True)
    )


def fill_mask(mask_ref, box_ref, clips):
    span = TOK // clips
    ids = lax.broadcasted_iota(jnp.int32, (span, BLOCK), 0)
    for clip in range(clips):
        low_f, high_f, low_r, high_r, low_c, high_c = (box_ref[6 * clip + k] for k in range(6))
        base = box_ref[6 * clips]
        frames = jnp.full((span, BLOCK), base, jnp.int32) if clips == 1 else ids >> 2
        patches = ids if clips == 1 else base + (ids & 3)
        rows, cols = patches >> 4, patches & 15
        within = (low_f <= frames) & (frames < high_f) & (low_r <= rows) & (rows < high_r) & (low_c <= cols) & (cols < high_c)
        mask_ref[clip * span : (clip + 1) * span, :] = jnp.where(within, 1.0, 0.0)


def picked_row(mod_ref, mask_ref, row):
    clips = mod_ref.shape[0]
    span = TOK // clips
    parts = []
    for clip in range(clips):
        inside_box = side([mask_ref[clip * span : (clip + 1) * span, :]] * (D // BLOCK)) > 0.5
        parts.append(
            jnp.where(
                inside_box,
                jnp.broadcast_to(mod_ref[clip, 1, row : row + 1, :], (span, D)),
                jnp.broadcast_to(mod_ref[clip, 0, row : row + 1, :], (span, D)),
            )
        )
    return parts[0] if clips == 1 else jnp.concatenate(parts, axis=0)


def fetch(slots_refs, where_ref, held, sem, base, row_tiles, col_tiles):
    step = 6

    def one(turn, carry):
        col = turn // (row_tiles // step)
        first = (turn % (row_tiles // step)) * step
        for k in range(step):
            row = first + k
            target = held.at[col, pl.ds(pl.multiple_of(row * BLOCK, BLOCK), BLOCK), :]
            place = where_ref[base + row * col_tiles + col]
            for ref, start, end in ((slots_refs[0], 0, 64 * BY_GATHER), (slots_refs[1], 64 * BY_GATHER, 64 * 14)):

                @pl.when(jnp.logical_and(place >= start, place < end))
                def _(ref=ref, start=start):
                    pltpu.make_async_copy(ref.at[place - start], target, sem).start()

        return carry

    lax.fori_loop(0, col_tiles * (row_tiles // step), one, 0)


def fetch_done(held, sem):
    pltpu.make_async_copy(held, held, sem).wait()


def forward_part(x, mod_ref, mask_ref, weights, waits, kept, same):
    wq, wo, w1, w2 = weights
    qkv_s, probs_s, attended_s, slope_s, active_s = kept
    lane = lax.broadcasted_iota(jnp.int32, (TOK, BLOCK), 1)
    low_half = lane < HD

    normal, _ = norm_parts(x)
    normed = (normal * (1.0 + picked_row(mod_ref, mask_ref, 1)) + picked_row(mod_ref, mask_ref, 0)).astype(bf16)
    waits[0]()

    def project(j, carry):
        qkv_s[j] = dot_nn(normed, side([wq[2 * j], wq[2 * j + 1]])).astype(bf16)
        return carry

    lax.fori_loop(0, 9, project, 0, unroll=True)

    def attend(c, carry):
        for pair in range(2):
            cols = slice(pair * BLOCK, (pair + 1) * BLOCK)
            q, k, v = qkv_s[c, :, cols], qkv_s[3 + c, :, cols], qkv_s[6 + c, :, cols]
            outs = []
            for e in range(2):
                mine = low_half if e == 0 else jnp.logical_not(low_half)
                scores = dot_nt(k, jnp.where(mine, q, jnp.zeros_like(q))) * HD ** (-0.5)
                if same is not None:
                    scores = jnp.where(same, scores, -jnp.inf)
                grown = jnp.exp(scores - jnp.max(scores, axis=0, keepdims=True))
                probs = (grown * (1.0 / jnp.sum(grown, axis=0, keepdims=True))).astype(bf16)
                probs_s[4 * c + 2 * pair + e] = probs
                outs.append(dot_tn(probs, v))
            attended_s[c, :, cols] = jnp.where(low_half, outs[0], outs[1]).astype(bf16)
        return carry

    lax.fori_loop(0, 3, attend, 0, unroll=True)
    attended = side([attended_s[c] for c in range(3)])
    waits[1]()
    branch = side([dot_nn(attended, side([wo[2 * j], wo[2 * j + 1]])) for j in range(3)])
    middle = x + picked_row(mod_ref, mask_ref, 2) * branch
    normal, _ = norm_parts(middle)
    renormed = (normal * (1.0 + picked_row(mod_ref, mask_ref, 4)) + picked_row(mod_ref, mask_ref, 3)).astype(bf16)
    waits[2]()

    def widen(j, carry):
        u = dot_nn(renormed, side([w1[2 * j], w1[2 * j + 1]]))
        root = (2.0 / 3.141592653589793) ** 0.5
        square = u * u
        bent = jnp.tanh(root * (u + 0.044715 * (square * u)))
        active_s[j] = (0.5 * u * (1.0 + bent)).astype(bf16)
        slope_s[j] = (
            0.5 * (1.0 + bent) + 0.5 * u * (1.0 - bent * bent) * (root * (1.0 + 3 * 0.044715 * square))
        ).astype(bf16)
        return carry

    lax.fori_loop(0, 12, widen, 0, unroll=True)
    active = side([active_s[j] for j in range(12)])
    waits[3]()
    mlp = side([dot_nn(active, side([w2[2 * j], w2[2 * j + 1]])) for j in range(3)])
    return middle, renormed, middle + picked_row(mod_ref, mask_ref, 5) * mlp


def send_tile(tile_ref, place, grads_refs, sem):
    start = 0
    for ref in grads_refs:
        size = ref.shape[0]

        @pl.when(jnp.logical_and(place >= start, place < start + size))
        def _(ref=ref, start=start):
            pltpu.make_async_copy(tile_ref, ref.at[place - start], sem).start()

        start += size


def send_tiles(stage, grads_refs, place_ref, sem, at, col_tiles, value, row, col):
    rows, cols = value.shape[0] // BLOCK, value.shape[1] // BLOCK
    for j in range(cols):
        for i in range(rows):
            tile = at + (row + i) * col_tiles + (col + j)
            stage[tile] = value[i * BLOCK : (i + 1) * BLOCK, j * BLOCK : (j + 1) * BLOCK].astype(bf16)
            send_tile(stage.at[tile], place_ref[tile], grads_refs, sem)


def backward_part(x, middle, renormed, upstream, mod_ref, mask_ref, weights, waits, kept, stage, grads_refs, place_ref, sem, acc, wide_s):
    wq, wo, w1, w2 = weights
    qkv_s, probs_s, attended_s, slope_s, active_s = kept
    lane = lax.broadcasted_iota(jnp.int32, (TOK, BLOCK), 1)
    low_half = lane < HD
    send = functools.partial(send_tiles, stage, grads_refs, place_ref, sem)

    grad_mlp = (picked_row(mod_ref, mask_ref, 5) * upstream).astype(bf16)
    renormed_t = renormed.T
    acc[...] = jnp.zeros_like(acc)
    waits[3]()
    waits[2]()

    def narrow(j, carry):
        rows = pl.ds(pl.multiple_of(j * CH, CH), CH)
        grad_active = dot_nt(grad_mlp, side([w2[n, rows, :] for n in range(6)]))
        grad_hidden = (grad_active * slope_s[j].astype(f32)).astype(bf16)
        acc[...] += dot_nt(grad_hidden, side([w1[2 * j], w1[2 * j + 1]]))
        send(FIRST_AT, 24, dot_nn(renormed_t, grad_hidden), 0, 2 * j)
        send(SECOND_AT, 6, dot_tn(active_s[j], grad_mlp), 2 * j, 0)
        return carry

    lax.fori_loop(0, 12, narrow, 0, unroll=True)
    normal, inverse = norm_parts(middle)
    grad_middle = upstream + norm_back(normal, inverse, (1.0 + picked_row(mod_ref, mask_ref, 4)) * acc[...])
    grad_branch = (picked_row(mod_ref, mask_ref, 2) * grad_middle).astype(bf16)
    waits[1]()

    def attend(c, carry):
        rows = pl.ds(pl.multiple_of(c * CH, CH), CH)
        grad_attended = dot_nt(grad_branch, side([wo[n, rows, :] for n in range(6)])).astype(bf16)
        send(OUT_AT, 6, dot_tn(attended_s[c], grad_branch), 2 * c, 0)
        for pair in range(2):
            cols = slice(pair * BLOCK, (pair + 1) * BLOCK)
            q, k, v = qkv_s[c, :, cols], qkv_s[3 + c, :, cols], qkv_s[6 + c, :, cols]
            ga = grad_attended[:, cols]
            grads = []
            for e in range(2):
                mine = low_half if e == 0 else jnp.logical_not(low_half)
                probs_low = probs_s[4 * c + 2 * pair + e]
                probs = probs_low.astype(f32)
                weighed = probs * dot_nt(v, jnp.where(mine, ga, jnp.zeros_like(ga)))
                grad_scores = (weighed - probs * jnp.sum(weighed, axis=0, keepdims=True)).astype(bf16)
                grads.append((dot_tn(grad_scores, k), dot_nn(grad_scores, q), dot_nn(probs_low, ga)))
            for n, scaling in ((0, HD ** (-0.5)), (1, HD ** (-0.5)), (2, 1.0)):
                wide_s[3 * n + c, :, cols] = (
                    jnp.where(low_half, grads[0][n], grads[1][n]) * scaling
                ).astype(bf16)
        return carry

    lax.fori_loop(0, 3, attend, 0, unroll=True)
    normal, inverse = norm_parts(x)
    scale_one = 1.0 + picked_row(mod_ref, mask_ref, 1)
    normed_t = (normal * scale_one + picked_row(mod_ref, mask_ref, 0)).astype(bf16).T
    acc[...] = jnp.zeros_like(acc)
    waits[0]()

    def gather_in(j, carry):
        piece = wide_s[j]
        acc[...] += dot_nt(piece, side([wq[2 * j], wq[2 * j + 1]]))
        send(QKV_AT, 18, dot_nn(normed_t, piece), 0, 2 * j)
        return carry

    lax.fori_loop(0, 9, gather_in, 0, unroll=True)
    normal, inverse = norm_parts(x)
    return grad_middle + norm_back(normal, inverse, scale_one * acc[...])


def same_sequence():
    rows = lax.broadcasted_iota(jnp.int32, (TOK, TOK), 0)
    cols = lax.broadcasted_iota(jnp.int32, (TOK, TOK), 1)
    return jnp.logical_and(rows // 64 == cols // 64, rows % 4 == cols % 4)


WEIGHT_SCRATCH = [
    pltpu.VMEM((18, D, BLOCK), bf16),
    pltpu.VMEM((6, D, BLOCK), bf16),
    pltpu.VMEM((24, D, BLOCK), bf16),
    pltpu.VMEM((6, FF, BLOCK), bf16),
    pltpu.SemaphoreType.DMA((4,)),
]
KEPT = [
    ((9, TOK, CH), bf16),
    ((HEADS, TOK, TOK), bf16),
    ((3, TOK, CH), bf16),
    ((12, TOK, CH), bf16),
    ((12, TOK, CH), bf16),
]
WEIGHT_RUNS = ((QKV_AT, 6, 18), (OUT_AT, 6, 6), (FIRST_AT, 6, 24), (SECOND_AT, 24, 6))


def fetch_all(slots_refs, where_ref, held, sems, base, order):
    for n in order:
        at, rows, cols = WEIGHT_RUNS[n]
        fetch(slots_refs, where_ref, held[n], sems.at[n], base + at, rows, cols)
    return [functools.partial(fetch_done, held[n], sems.at[n]) for n in range(4)]


def first_forward(where_ref, box_ref, x_ref, mods_ref, gathered_ref, passed_ref, middle_ref, out_ref, *rest):
    mask_ref, rest = rest[-1], rest[:-1]
    fill_mask(mask_ref, box_ref, 1)
    mod_ref = mods_ref.at[pl.ds(box_ref[7], 1), 0]
    kept, (wq, wo, w1, w2, sems) = rest[:5], rest[5:]
    weights = (wq, wo, w1, w2)
    waits = fetch_all((gathered_ref, passed_ref), where_ref, weights, sems, 0, (0, 1, 2, 3))
    middle, _, output = forward_part(x_ref[...].astype(f32), mod_ref, mask_ref, weights, waits, kept, None)
    middle_ref[...] = middle
    out_ref[...] = output.astype(bf16)


def second_layer(
    where_ref, place_ref, box_ref, x_ref, up_ref, mods_ref, gathered_ref, passed_ref, out_ref, grad_ref, *rest
):
    mask_ref, rest = rest[-1], rest[:-1]
    fill_mask(mask_ref, box_ref, 4)
    mod_ref = mods_ref.at[:, 1]
    grads_refs, rest = rest[:6], rest[6:]
    kept, (wq, wo, w1, w2, sems, stage, sem, acc, wide_s) = rest[:5], rest[5:]
    weights = (wq, wo, w1, w2)
    waits = fetch_all((gathered_ref, passed_ref), where_ref, weights, sems, LAYER_TILES, (0, 1, 2, 3))
    x = x_ref[...].astype(f32)
    middle, renormed, output = forward_part(x, mod_ref, mask_ref, weights, waits, kept, same_sequence())
    out_ref[...] = output.astype(bf16)
    nothing = [lambda: None] * 4
    grad = backward_part(
        x, middle, renormed, up_ref[...].astype(f32), mod_ref, mask_ref, weights, nothing, kept,
        stage, grads_refs, place_ref.at[pl.ds(LAYER_TILES, LAYER_TILES)], sem, acc, wide_s,
    )
    grad_ref[...] = grad.astype(bf16)
    pltpu.make_async_copy(stage, stage, sem).wait()


def first_backward(
    where_ref, place_ref, box_ref, x_ref, middle_ref, up_ref, mods_ref, gathered_ref, passed_ref,
    qkv_s, probs_s, attended_s, slope_s, active_s, *rest,
):
    mask_ref, rest = rest[-1], rest[:-1]
    fill_mask(mask_ref, box_ref, 1)
    mod_ref = mods_ref.at[pl.ds(box_ref[7], 1), 0]
    grad_ref, *grads_refs = rest[6:13]
    wq, wo, w1, w2, sems, stage, sem, acc, wide_s = rest[13:]
    weights = (wq, wo, w1, w2)
    waits = fetch_all((gathered_ref, passed_ref), where_ref, weights, sems, 0, (3, 2, 1, 0))
    x, middle = x_ref[...].astype(f32), middle_ref[...]
    normal, _inverse = norm_parts(middle)
    renormed = (normal * (1.0 + picked_row(mod_ref, mask_ref, 4)) + picked_row(mod_ref, mask_ref, 3)).astype(bf16)
    grad = backward_part(
        x, middle, renormed, up_ref[...].astype(f32), mod_ref, mask_ref, weights, waits,
        (qkv_s, probs_s, attended_s, slope_s, active_s), stage, grads_refs, place_ref, sem, acc, wide_s,
    )
    grad_ref[...] = grad.astype(bf16)
    pltpu.make_async_copy(stage, stage, sem).wait()


SMEM = pl.BlockSpec(memory_space=pltpu.SMEM)
VMEM = pl.BlockSpec(memory_space=pltpu.VMEM)
ANY = pl.BlockSpec(memory_space=pl.ANY)
MASK = pltpu.VMEM((TOK, BLOCK), f32)
PARAMS = pltpu.CompilerParams(vmem_limit_bytes=60 * 1024 * 1024)
BACK_SCRATCH = [
    pltpu.VMEM((LAYER_TILES, BLOCK, BLOCK), bf16),
    pltpu.SemaphoreType.DMA,
    pltpu.VMEM((TOK, D), f32),
    pltpu.VMEM((9, TOK, CH), bf16),
]


PARTS = (140, 112, 196)
GRADS = [jax.ShapeDtypeStruct((n, BLOCK, BLOCK), bf16) for n in PARTS + PARTS]


def run_first_forward(where, box, x, mods, slots):
    return pl.pallas_call(
        first_forward,
        name="first_forward",
        out_shape=[jax.ShapeDtypeStruct((TOK, D), f32), jax.ShapeDtypeStruct((TOK, D), bf16)]
        + [jax.ShapeDtypeStruct(s, t) for s, t in KEPT],
        in_specs=[SMEM, SMEM, VMEM, VMEM, ANY, ANY],
        out_specs=[VMEM] * 7,
        scratch_shapes=WEIGHT_SCRATCH + [MASK],
        compiler_params=PARAMS,
    )(where, box, x, mods, *slots)


def run_second(where, place, box, x, up, mods, slots):
    return pl.pallas_call(
        second_layer,
        name="second_layer",
        out_shape=[
            jax.ShapeDtypeStruct((TOK, D), bf16),
            jax.ShapeDtypeStruct((TOK, D), bf16),
            *GRADS,
        ],
        in_specs=[SMEM, SMEM, SMEM, VMEM, VMEM, VMEM, ANY, ANY],
        out_specs=[VMEM, VMEM] + [ANY] * 6,
        scratch_shapes=[pltpu.VMEM(s, t) for s, t in KEPT] + WEIGHT_SCRATCH + BACK_SCRATCH + [MASK],
        compiler_params=PARAMS,
    )(where, place, box, x, up, mods, *slots)


def run_first_backward(where, place, box, x, middle, up, mods, slots, kept, grads):
    return pl.pallas_call(
        first_backward,
        name="first_backward",
        out_shape=[
            jax.ShapeDtypeStruct((TOK, D), bf16),
            *GRADS,
        ],
        in_specs=[SMEM] * 3 + [VMEM] * 4 + [ANY] * 2 + [VMEM] * 5 + [ANY] * 6,
        out_specs=[VMEM] + [ANY] * 6,
        scratch_shapes=WEIGHT_SCRATCH + BACK_SCRATCH + [MASK],
        input_output_aliases={14 + k: 1 + k for k in range(6)},
        compiler_params=PARAMS,
    )(where, place, box, x, middle, up, mods, *slots, *kept, *grads)


def everyone():
    for y in range(4):
        for xh in range(2):
            for z in range(4):
                for c in range(2):
                    for xl in range(2):
                        yield (y, xh, z, c, xl)


def number(y, xh, z, c, xl):
    return (((y * 2 + xh) * 4 + z) * 2 + c) * 2 + xl


def permute(value, target):
    return lax.ppermute(value, EVERY, [(number(*d), number(*target(*d))) for d in everyone()])


def along(axis, step):
    def target(y, xh, z, c, xl):
        if (axis == 0) == (c == 0):
            return ((y + step) % 4, xh, z, c, xl)
        return (y, xh, (z + step) % 4, c, xl)

    return target


def other_core(y, xh, z, c, xl):
    return (y, xh, z, 1 - c, xl)


def across(y, xh, z, c, xl):
    return (y, 1 - xh, z, c, 1 - xl)


def twin(y, xh, z, c, xl):
    return (y, xh, z, c, 1 - xl)


def added(*values):
    total = values[0].astype(f32)
    for value in values[1:]:
        total = total + value.astype(f32)
    return total.astype(bf16)


def pair(y, xh, z, c, xl):
    return twin(y, xh, z, c, xl) if c == 0 else across(y, xh, z, c, xl)


def opposite(y, xh, z, c, xl):
    return (y, 1 - xh, z, c, xl)


def pair_last(y, xh, z, c, xl):
    return across(y, xh, z, c, xl) if c == 0 else twin(y, xh, z, c, xl)


PIECES = {
    "plain2": (0, 56), "given2": (56, 28), "given13": (84, 56), "plain13": (140, 112), "kept2": (252, 28),
    "kept13": (280, 56), "given0": (336, 28), "kept0": (364, 28), "plain0": (392, 56),
}
TILE_STEP = 7


def add_tiles(plan, source_count, last_count, *refs):
    sources, outs = refs[:source_count], refs[source_count + last_count :]
    for out, parts in zip(outs, plan):
        for at, size, terms in parts:
            step = TILE_STEP if size % TILE_STEP == 0 else size

            def some(i, carry, out=out, at=at, terms=terms, step=step):
                for k in range(step):
                    n = i * step + k
                    total = sources[terms[0][0]][terms[0][1] + n].astype(f32)
                    for source, start in terms[1:]:
                        total = total + sources[source][start + n].astype(f32)
                    out[at + n] = total.astype(bf16)
                return carry

            lax.fori_loop(0, size // step, some, 0)


def keep(*refs):
    pass


FREE = pl.CostEstimate(flops=1, bytes_accessed=1, transcendentals=0)


class TileSums:
    def __init__(self):
        self.last = []

    def __call__(self, plan, *sources, after=()):
        sizes = [sum(size for _, size, _ in parts) for parts in plan]
        last = [*self.last, *after]
        tiles = sum(sizes) + sum(value.shape[0] for value in sources)
        outs = pl.pallas_call(
            functools.partial(add_tiles, plan, len(sources), len(last)),
            name="add_tiles",
            out_shape=[jax.ShapeDtypeStruct((n, BLOCK, BLOCK), bf16) for n in sizes]
            + [jax.ShapeDtypeStruct((8, BLOCK), f32)],
            in_specs=[VMEM] * len(sources) + [ANY] * len(last),
            out_specs=[VMEM] * len(sizes) + [ANY],
            compiler_params=pltpu.CompilerParams(vmem_limit_bytes=tiles * 32768 + 1024 * 1024),
            cost_estimate=FREE,
        )(*sources, *last)
        self.last = [outs[-1]]
        return outs[:-1]


def then(value, *last):
    return pl.pallas_call(
        keep,
        name="keep",
        out_shape=jax.ShapeDtypeStruct(value.shape, value.dtype),
        in_specs=[ANY] * (1 + len(last)),
        out_specs=ANY,
        input_output_aliases={0: 0},
        cost_estimate=FREE,
    )(value, *last)


def reduce_tiles(mine, given, core, frame, token_blocks, send_tokens, renew):
    add = TileSums()
    at = {name: start for name, (start, _) in PIECES.items()}

    def alone(size, *terms):
        return [(0, size, list(terms))]

    got = permute(given[0], other_core)
    p2_a, p2_b, over = add(
        [alone(28, (0, 0), (1, 0)), alone(28, (0, 28), (1, 28)), alone(84, (0, 56), (1, 56))], mine[0], got
    )
    p2_ahead, p2_behind = permute(p2_a, along(0, 1)), permute(p2_b, along(0, -1))
    x213 = permute(over, pair)
    got = permute(then(given[1], *add.last), other_core)
    last_got = permute(then(given[2], *add.last), other_core)
    p13 = add(
        [
            [(0, 28, [(0, 0), (1, 0), (2, 0)]), (28, 28, [(0, 28), (1, 28)])],
            [(0, 28, [(0, 56), (1, 56)]), (28, 28, [(0, 84), (1, 84), (3, 0)])],
        ],
        mine[1], got, p2_ahead, p2_behind,
    )
    p1, p3 = permute(p13[0], along(0, 1)), permute(p13[1], along(0, -1))
    mine, got = mine[2], last_got
    at = {name: start - 252 for name, start in at.items()}
    x0 = permute(add([alone(28, (0, at["given0"]), (1, at["given0"]))], mine, got)[0], pair)
    h2 = add([alone(14, (0, at["kept2"] + n), (1, at["kept2"] + n), (2, n)) for n in (0, 14)], mine, got, x213)
    h2_ahead, h2_behind = permute(h2[0], along(0, 1)), permute(h2[1], along(0, -1))

    def split(start, cuts):
        return [
            alone(size, (0, start + n), (1, start + n), *((k, n) for k in more)) for n, size, more in cuts
        ]

    p = add(
        split(at["plain0"], [(28, 7, (2, 3)), (35, 7, (2, 3)), (0, 14, (2, 3)), (14, 14, (2, 3)), (42, 14, (2, 3))]),
        mine, got, p1, p3,
    )
    ahead, behind = permute(p[0], along(1, 1)), permute(p[1], along(1, -1))
    k13 = r13 = at["kept13"]
    h13 = add(
        [
            [(0, 14, [(0, k13), (1, r13), (2, 28), (3, 0)]), (14, 14, [(0, k13 + 14), (1, r13 + 14), (2, 42)])],
            [(0, 14, [(0, k13 + 28), (1, r13 + 28), (2, 56)]), (14, 14, [(0, k13 + 42), (1, r13 + 42), (2, 70), (4, 0)])],
        ],
        mine, got, x213, h2_ahead, h2_behind,
    )
    h1, h3 = permute(h13[0], along(0, 1)), permute(h13[1], along(0, -1))
    sides = add(
        [
            [(0, 7, [(0, 0), (1, 0)]), (7, 7, [(0, 7)])],
            [(0, 7, [(2, 0)]), (7, 7, [(2, 7), (3, 0)])],
        ],
        p[3], ahead, p[4], behind,
    )
    up, down = permute(sides[0], along(1, 1)), permute(sides[1], along(1, -1))
    h = add(
        split(at["kept0"], [(14, 4, (2, 3, 4)), (18, 3, (2, 3, 4)), (0, 7, (2, 3, 4)), (7, 7, (2, 3, 4)), (21, 7, (2, 3, 4))]),
        mine, got, x0, h1, h3,
    )
    h_ahead, h_behind = permute(h[0], along(1, 1)), permute(h[1], along(1, -1))
    token_blocks = send_tokens(then(token_blocks, *add.last))
    p = add([alone(7, (0, n), (1, n), (2, n)) for n in (0, 7)], p[2], up, down)
    far = permute(p[1], across)
    sides = add(
        [
            [(0, 4, [(0, 0), (1, 0)]), (4, 3, [(0, 4)])],
            [(0, 4, [(2, 0)]), (4, 3, [(2, 4), (3, 0)])],
        ],
        h[3], h_ahead, h[4], h_behind,
    )
    h_up, h_down = permute(sides[0], along(1, 1)), permute(sides[1], along(1, -1))
    (p,) = add([alone(7, (0, 0), (1, 0))], p[0], far)
    match = permute(p, twin)
    (h,) = add([alone(7, (0, 0), (1, 0), (2, 0))], h[2], h_up, h_down, after=[token_blocks])
    beyond, beside, around = permute(h, pair_last), permute(h, twin), permute(h, opposite)
    told = (core == 0) & (frame == 1)
    h = added(jnp.where(told, beside, h), jnp.where(told, around, beyond))
    renewed = renew([p, match])
    return renewed, permute(then(h, renewed[0]), other_core), token_blocks


def precondition(term_count, info_ref, *refs):
    terms, refs = refs[:term_count], refs[term_count:]
    sources, refs = refs[:5], refs[-14:]
    outs, held, made, sems = refs[:4], refs[4:9], refs[9:13], refs[13]
    start = info_ref[0]
    loads = [
        pltpu.make_async_copy(source.at[pl.ds(start, 7)], here, sems.at[n])
        for n, (source, here) in enumerate(zip(sources, held))
    ]
    for load in loads:
        load.start()
    for load in loads:
        load.wait()
    masters, left_stats, right_stats, left_roots, right_roots = held
    grads, new_left, new_right, new_masters = made

    def product(a, b, dims):
        return lax.dot_general(a, b, (dims, ((), ())), preferred_element_type=f32, precision=highest)

    for n in range(7):
        total = terms[0][n].astype(f32)
        for term in terms[1:]:
            total = total + term[n].astype(f32)
        grad = jnp.where(info_ref[1 + start + n] > 0, total, 0.0)
        grads[n] = grad
        new_left[n] = stat_decay * left_stats[n] + (1.0 - stat_decay) * product(grad, grad, ((1,), (1,)))
        new_right[n] = stat_decay * right_stats[n] + (1.0 - stat_decay) * product(grad, grad, ((0,), (0,)))
        rotated = product(grad, right_roots[n], ((1,), (0,)))
        new_masters[n] = masters[n] - learning_rate * product(left_roots[n], rotated, ((1,), (0,)))
    stores = [
        pltpu.make_async_copy(here, out.at[pl.ds(start, 7)], sems.at[n]) for n, (here, out) in enumerate(zip(made, outs))
    ]
    for store in stores:
        store.start()
    for store in stores:
        store.wait()


def run_precondition(info, terms, sources, outs):
    seven = pltpu.VMEM((7, BLOCK, BLOCK), f32)
    return pl.pallas_call(
        functools.partial(precondition, len(terms)),
        name="precondition",
        out_shape=[jax.ShapeDtypeStruct((14, BLOCK, BLOCK), f32)] * 4,
        in_specs=[SMEM] + [VMEM] * len(terms) + [ANY] * (5 + len(outs)),
        out_specs=[ANY] * 4,
        scratch_shapes=[seven] * 9 + [pltpu.SemaphoreType.DMA((5,))],
        input_output_aliases={6 + len(terms) + k: k for k in range(len(outs))},
        compiler_params=pltpu.CompilerParams(vmem_limit_bytes=16 * 1024 * 1024),
        cost_estimate=pl.CostEstimate(flops=7 * 4 * 6 * 2 * BLOCK**3, bytes_accessed=7 * 9 * 65536, transcendentals=0),
    )(info, *terms, *sources, *outs)


BY_GATHER = 7
OTHERS = 14 - BY_GATHER


def gather_tiles(tiles, beside):
    gathered = lax.all_gather(tiles[:BY_GATHER], POS, axis=0, tiled=True)
    here, n = tiles[BY_GATHER:], OTHERS
    base = jnp.concatenate([here, permute(here, across)], axis=0)
    behind, ahead = permute(base, along(1, 1)), permute(base, along(1, -1))
    far = [permute(behind[:n], along(1, 1)), permute(ahead[n:], along(1, -1))]
    own = jnp.concatenate([base, behind, ahead, *far], axis=0)
    behind, ahead = permute(own, along(0, 1)), permute(own, along(0, -1))
    far = [permute(behind[: 4 * n], along(0, 1)), permute(ahead[4 * n :], along(0, -1))]
    near = jnp.concatenate([own, behind, ahead], axis=0)
    far = then(jnp.concatenate(far, axis=0), *beside)
    passed = jnp.concatenate([near, far, permute(near, other_core), permute(far, other_core)], axis=0)
    return gathered, passed


def source_of(slots, y, xh, z, core):
    owner, k = slots // 14, slots % 14
    owner_y, owner_xh, owner_z, owner_c = owner // 16, owner // 8 % 2, owner // 2 % 4, owner % 2
    ahead_y, ahead_z = (owner_y - y) % 4, (owner_z - z) % 4
    first = jnp.where(owner_c == 0, ahead_y, ahead_z)
    second = jnp.where(owner_c == 0, ahead_z, ahead_y)

    def rank(ring):
        return jnp.where(ring == 3, 1, jnp.where(ring == 1, 2, jnp.where(ring == 2, 3, 0)))

    place = (((owner_c + core) % 2 * 4 + rank(first)) * 4 + rank(second)) * 2 + (owner_xh + xh) % 2
    place = 64 * BY_GATHER + place * OTHERS + k - BY_GATHER
    return jnp.where(k < BY_GATHER, owner * BY_GATHER + k, place).astype(jnp.int32)


def place_of(slots, y, xh, z, core, frame):
    owner, k = slots // 14, slots % 14
    owner_y, owner_xh, owner_z, owner_c = owner // 16, owner // 8 % 2, owner // 2 % 4, owner % 2
    handler = k // 7
    ahead_y, ahead_z = (owner_y - y) % 4, (owner_z - z) % 4
    first = jnp.where(handler == 0, ahead_y, ahead_z)
    second = jnp.where(handler == 0, ahead_z, ahead_y)
    over_x = (owner_xh + xh) % 2
    kept = jnp.where(handler == 0, (over_x + frame) % 2, over_x) == 0

    def start(prefix, size):
        at0, at2, at13 = (PIECES[prefix + ring][0] for ring in ("0", "2", "13"))
        return jnp.where(first == 0, at0, jnp.where(first == 2, at2, at13 + size * (first // 2)))

    plain = start("plain", 56) + (second * 2 + over_x) * 7
    halved = jnp.where(kept, start("kept", 28), start("given", 28)) + second * 7
    place = jnp.where(owner_c == handler, plain, halved) + k % 7
    return ((handler + core) % 2 * 448 + place).astype(jnp.int32)


def local(
    tokens,
    modulation,
    box_bounds,
    masters,
    left_stats,
    right_stats,
    left_roots,
    right_roots,
    owner_slot,
    cotangent,
):
    y, xh, z, core = (lax.axis_index(a) for a in POS)
    mine, copy = lax.axis_index(POS), lax.axis_index("frame")

    def to_frames(value):
        return lax.all_to_all(value.reshape(64, 4, D), POS, 0, 0, tiled=True).reshape(TOK, D)

    clip, frame = mine // 16, mine % 16
    bounds_here = lax.dynamic_index_in_dim(box_bounds, clip, 0, keepdims=False)
    box_first = jnp.concatenate([bounds_here, jnp.stack([frame, clip])]).astype(jnp.int32)
    box_second = jnp.concatenate([box_bounds.reshape(24), jnp.stack([mine * 4])]).astype(jnp.int32)
    where = source_of(owner_slot, y, xh, z, core)
    place = place_of(owner_slot, y, xh, z, core, copy)
    upstream = cotangent.reshape(TOK, D)
    tokens_here = to_frames(tokens)
    slots = gather_tiles(masters.astype(bf16), [tokens_here, where, place])
    middle, passed, *kept = run_first_forward(where, box_first, tokens_here, modulation, slots)
    here = to_frames(passed)
    block_output, grad_here, *grads = run_second(where, place, box_second, here, upstream, modulation, slots)
    upstream = to_frames(grad_here)
    token_grads, *grads = run_first_backward(
        where, place, box_first, tokens_here, middle, upstream, modulation, slots, kept, grads
    )
    slot_ids = mine * 14 + jnp.arange(14, dtype=jnp.int32)
    holds = jnp.any(owner_slot[None, :] == slot_ids[:, None], axis=1)
    sources = [masters, left_stats, right_stats, left_roots, right_roots]

    def info(start):
        return jnp.concatenate([jnp.stack([start]), holds]).astype(jnp.int32)

    def renew(terms):
        return run_precondition(info(core * 7), terms, sources, [])

    renewed, halved, token_grads = reduce_tiles(grads[:3], grads[3:], core, copy, token_grads, to_frames, renew)
    renewed = run_precondition(info(7 - core * 7), [halved], sources, renewed)
    return (block_output.reshape(tokens.shape), token_grads.reshape(tokens.shape), *renewed)


def solution(mesh):
    split = Mesh(
        mesh.devices.reshape(4, 2, 4, 2, mesh.shape["frame"]),
        ("pos_0", "pos_1", "pos_2", "pos_3", "frame"),
    )
    return jax.shard_map(
        local,
        mesh=split,
        in_specs=(
            P("frame", None, POS, None),
            P("frame", None, None, None, None),
            P("frame", None),
            P(POS, None, None),
            P(POS, None, None),
            P(POS, None, None),
            P(POS, None, None),
            P(POS, None, None),
            P(),
            P("frame", None, POS, None),
        ),
        out_specs=(
            P("frame", None, POS, None),
            P("frame", None, POS, None),
            P(POS, None, None),
            P(POS, None, None),
            P(POS, None, None),
            P(POS, None, None),
        ),
        check_vma=False,
    )
```

```python
import functools

import jax
import jax.numpy as jnp
from jax import lax
from jax.experimental import pallas as pl
from jax.experimental.pallas import tpu as pltpu
from jax.sharding import Mesh
from jax.sharding import PartitionSpec as P

D = 768
HEADS = 12
HD = 64
FF = 3072
GRID = 16
BLOCK = 128
TOK = 256
CH = 256
POS = ("pos_0", "pos_1", "pos_2", "pos_3")
EVERY = ("pos_0", "pos_1", "pos_2", "pos_3", "frame")

highest = lax.Precision.HIGHEST
stat_decay = 0.5
learning_rate = 0.7
norm_epsilon = 1e-06
f32 = jnp.float32
bf16 = jnp.bfloat16

QKV_AT, OUT_AT, FIRST_AT, SECOND_AT, LAYER_TILES = 0, 108, 144, 288, 432


def dot_nn(a, b):
    return lax.dot_general(a, b, (((1,), (0,)), ((), ())), preferred_element_type=f32)


def dot_nt(a, b):
    return lax.dot_general(a, b, (((1,), (1,)), ((), ())), preferred_element_type=f32)


def dot_tn(a, b):
    return lax.dot_general(a, b, (((0,), (0,)), ((), ())), preferred_element_type=f32)


def side(parts):
    return jnp.concatenate(parts, axis=1)


def norm_parts(values):
    center = values - jnp.mean(values, axis=-1, keepdims=True)
    spread = jnp.mean(center * center, axis=-1, keepdims=True)
    inverse = lax.rsqrt(spread + norm_epsilon)
    return center * inverse, inverse


def norm_back(normal, inverse, grad):
    return inverse * (
        grad
        - jnp.mean(grad, axis=-1, keepdims=True)
        - normal * jnp.mean(grad * normal, axis=-1, keepdims=True)
    )


def fill_mask(mask_ref, box_ref, clips):
    span = TOK // clips
    ids = lax.broadcasted_iota(jnp.int32, (span, BLOCK), 0)
    for clip in range(clips):
        low_f, high_f, low_r, high_r, low_c, high_c = (box_ref[6 * clip + k] for k in range(6))
        base = box_ref[6 * clips]
        frames = jnp.full((span, BLOCK), base, jnp.int32) if clips == 1 else ids >> 2
        patches = ids if clips == 1 else base + (ids & 3)
        rows, cols = patches >> 4, patches & 15
        within = (low_f <= frames) & (frames < high_f) & (low_r <= rows) & (rows < high_r) & (low_c <= cols) & (cols < high_c)
        mask_ref[clip * span : (clip + 1) * span, :] = jnp.where(within, 1.0, 0.0)


def picked_row(mod_ref, mask_ref, row):
    clips = mod_ref.shape[0]
    span = TOK // clips
    parts = []
    for clip in range(clips):
        inside_box = side([mask_ref[clip * span : (clip + 1) * span, :]] * (D // BLOCK)) > 0.5
        parts.append(
            jnp.where(
                inside_box,
                jnp.broadcast_to(mod_ref[clip, 1, row : row + 1, :], (span, D)),
                jnp.broadcast_to(mod_ref[clip, 0, row : row + 1, :], (span, D)),
            )
        )
    return parts[0] if clips == 1 else jnp.concatenate(parts, axis=0)


def fetch(slots_refs, where_ref, held, sem, base, row_tiles, col_tiles):
    step = 6

    def one(turn, carry):
        col = turn // (row_tiles // step)
        first = (turn % (row_tiles // step)) * step
        for k in range(step):
            row = first + k
            target = held.at[col, pl.ds(pl.multiple_of(row * BLOCK, BLOCK), BLOCK), :]
            place = where_ref[base + row * col_tiles + col]
            for ref, start, end in ((slots_refs[0], 0, 64 * BY_GATHER), (slots_refs[1], 64 * BY_GATHER, 64 * 14)):

                @pl.when(jnp.logical_and(place >= start, place < end))
                def _(ref=ref, start=start):
                    pltpu.make_async_copy(ref.at[place - start], target, sem).start()

        return carry

    lax.fori_loop(0, col_tiles * (row_tiles // step), one, 0)


def fetch_done(held, sem):
    pltpu.make_async_copy(held, held, sem).wait()


def forward_part(x, mod_ref, mask_ref, weights, waits, kept, same):
    wq, wo, w1, w2 = weights
    qkv_s, probs_s, attended_s, slope_s, active_s = kept
    lane = lax.broadcasted_iota(jnp.int32, (TOK, BLOCK), 1)
    low_half = lane < HD

    normal, _ = norm_parts(x)
    normed = (normal * (1.0 + picked_row(mod_ref, mask_ref, 1)) + picked_row(mod_ref, mask_ref, 0)).astype(bf16)
    waits[0]()

    def project(j, carry):
        qkv_s[j] = dot_nn(normed, side([wq[2 * j], wq[2 * j + 1]])).astype(bf16)
        return carry

    lax.fori_loop(0, 9, project, 0, unroll=True)

    def attend(c, carry):
        for pair in range(2):
            cols = slice(pair * BLOCK, (pair + 1) * BLOCK)
            q, k, v = qkv_s[c, :, cols], qkv_s[3 + c, :, cols], qkv_s[6 + c, :, cols]
            outs = []
            for e in range(2):
                mine = low_half if e == 0 else jnp.logical_not(low_half)
                scores = dot_nt(k, jnp.where(mine, q, jnp.zeros_like(q))) * HD ** (-0.5)
                if same is not None:
                    scores = jnp.where(same, scores, -jnp.inf)
                grown = jnp.exp(scores - jnp.max(scores, axis=0, keepdims=True))
                probs = (grown * (1.0 / jnp.sum(grown, axis=0, keepdims=True))).astype(bf16)
                probs_s[4 * c + 2 * pair + e] = probs
                outs.append(dot_tn(probs, v))
            attended_s[c, :, cols] = jnp.where(low_half, outs[0], outs[1]).astype(bf16)
        return carry

    lax.fori_loop(0, 3, attend, 0, unroll=True)
    attended = side([attended_s[c] for c in range(3)])
    waits[1]()
    branch = side([dot_nn(attended, side([wo[2 * j], wo[2 * j + 1]])) for j in range(3)])
    middle = x + picked_row(mod_ref, mask_ref, 2) * branch
    normal, _ = norm_parts(middle)
    renormed = (normal * (1.0 + picked_row(mod_ref, mask_ref, 4)) + picked_row(mod_ref, mask_ref, 3)).astype(bf16)
    waits[2]()

    def widen(j, carry):
        u = dot_nn(renormed, side([w1[2 * j], w1[2 * j + 1]]))
        root = (2.0 / 3.141592653589793) ** 0.5
        square = u * u
        bent = jnp.tanh(root * (u + 0.044715 * (square * u)))
        active_s[j] = (0.5 * u * (1.0 + bent)).astype(bf16)
        slope_s[j] = (
            0.5 * (1.0 + bent) + 0.5 * u * (1.0 - bent * bent) * (root * (1.0 + 3 * 0.044715 * square))
        ).astype(bf16)
        return carry

    lax.fori_loop(0, 12, widen, 0, unroll=True)
    active = side([active_s[j] for j in range(12)])
    waits[3]()
    mlp = side([dot_nn(active, side([w2[2 * j], w2[2 * j + 1]])) for j in range(3)])
    return middle, renormed, middle + picked_row(mod_ref, mask_ref, 5) * mlp


def send_tile(tile_ref, place, grads_refs, sem):
    start = 0
    for ref in grads_refs:
        size = ref.shape[0]

        @pl.when(jnp.logical_and(place >= start, place < start + size))
        def _(ref=ref, start=start):
            pltpu.make_async_copy(tile_ref, ref.at[place - start], sem).start()

        start += size


def send_tiles(stage, grads_refs, place_ref, sem, at, col_tiles, value, row, col):
    rows, cols = value.shape[0] // BLOCK, value.shape[1] // BLOCK
    for j in range(cols):
        for i in range(rows):
            tile = at + (row + i) * col_tiles + (col + j)
            stage[tile] = value[i * BLOCK : (i + 1) * BLOCK, j * BLOCK : (j + 1) * BLOCK].astype(bf16)
            send_tile(stage.at[tile], place_ref[tile], grads_refs, sem)


def backward_part(x, middle, renormed, upstream, mod_ref, mask_ref, weights, waits, kept, stage, grads_refs, place_ref, sem, acc, wide_s):
    wq, wo, w1, w2 = weights
    qkv_s, probs_s, attended_s, slope_s, active_s = kept
    lane = lax.broadcasted_iota(jnp.int32, (TOK, BLOCK), 1)
    low_half = lane < HD
    send = functools.partial(send_tiles, stage, grads_refs, place_ref, sem)

    grad_mlp = (picked_row(mod_ref, mask_ref, 5) * upstream).astype(bf16)
    renormed_t = renormed.T
    acc[...] = jnp.zeros_like(acc)
    waits[3]()
    waits[2]()

    def narrow(j, carry):
        rows = pl.ds(pl.multiple_of(j * CH, CH), CH)
        grad_active = dot_nt(grad_mlp, side([w2[n, rows, :] for n in range(6)]))
        grad_hidden = (grad_active * slope_s[j].astype(f32)).astype(bf16)
        acc[...] += dot_nt(grad_hidden, side([w1[2 * j], w1[2 * j + 1]]))
        send(FIRST_AT, 24, dot_nn(renormed_t, grad_hidden), 0, 2 * j)
        send(SECOND_AT, 6, dot_tn(active_s[j], grad_mlp), 2 * j, 0)
        return carry

    lax.fori_loop(0, 12, narrow, 0, unroll=True)
    normal, inverse = norm_parts(middle)
    grad_middle = upstream + norm_back(normal, inverse, (1.0 + picked_row(mod_ref, mask_ref, 4)) * acc[...])
    grad_branch = (picked_row(mod_ref, mask_ref, 2) * grad_middle).astype(bf16)
    waits[1]()

    def attend(c, carry):
        rows = pl.ds(pl.multiple_of(c * CH, CH), CH)
        grad_attended = dot_nt(grad_branch, side([wo[n, rows, :] for n in range(6)])).astype(bf16)
        send(OUT_AT, 6, dot_tn(attended_s[c], grad_branch), 2 * c, 0)
        for pair in range(2):
            cols = slice(pair * BLOCK, (pair + 1) * BLOCK)
            q, k, v = qkv_s[c, :, cols], qkv_s[3 + c, :, cols], qkv_s[6 + c, :, cols]
            ga = grad_attended[:, cols]
            grads = []
            for e in range(2):
                mine = low_half if e == 0 else jnp.logical_not(low_half)
                probs_low = probs_s[4 * c + 2 * pair + e]
                probs = probs_low.astype(f32)
                weighed = probs * dot_nt(v, jnp.where(mine, ga, jnp.zeros_like(ga)))
                grad_scores = (weighed - probs * jnp.sum(weighed, axis=0, keepdims=True)).astype(bf16)
                grads.append((dot_tn(grad_scores, k), dot_nn(grad_scores, q), dot_nn(probs_low, ga)))
            for n, scaling in ((0, HD ** (-0.5)), (1, HD ** (-0.5)), (2, 1.0)):
                wide_s[3 * n + c, :, cols] = (
                    jnp.where(low_half, grads[0][n], grads[1][n]) * scaling
                ).astype(bf16)
        return carry

    lax.fori_loop(0, 3, attend, 0, unroll=True)
    normal, inverse = norm_parts(x)
    scale_one = 1.0 + picked_row(mod_ref, mask_ref, 1)
    normed_t = (normal * scale_one + picked_row(mod_ref, mask_ref, 0)).astype(bf16).T
    acc[...] = jnp.zeros_like(acc)
    waits[0]()

    def gather_in(j, carry):
        piece = wide_s[j]
        acc[...] += dot_nt(piece, side([wq[2 * j], wq[2 * j + 1]]))
        send(QKV_AT, 18, dot_nn(normed_t, piece), 0, 2 * j)
        return carry

    lax.fori_loop(0, 9, gather_in, 0, unroll=True)
    normal, inverse = norm_parts(x)
    return grad_middle + norm_back(normal, inverse, scale_one * acc[...])


def same_sequence():
    rows = lax.broadcasted_iota(jnp.int32, (TOK, TOK), 0)
    cols = lax.broadcasted_iota(jnp.int32, (TOK, TOK), 1)
    return jnp.logical_and(rows // 64 == cols // 64, rows % 4 == cols % 4)


WEIGHT_SCRATCH = [
    pltpu.VMEM((18, D, BLOCK), bf16),
    pltpu.VMEM((6, D, BLOCK), bf16),
    pltpu.VMEM((24, D, BLOCK), bf16),
    pltpu.VMEM((6, FF, BLOCK), bf16),
    pltpu.SemaphoreType.DMA((4,)),
]
KEPT = [
    ((9, TOK, CH), bf16),
    ((HEADS, TOK, TOK), bf16),
    ((3, TOK, CH), bf16),
    ((12, TOK, CH), bf16),
    ((12, TOK, CH), bf16),
]
WEIGHT_RUNS = ((QKV_AT, 6, 18), (OUT_AT, 6, 6), (FIRST_AT, 6, 24), (SECOND_AT, 24, 6))


def fetch_all(slots_refs, where_ref, held, sems, base, order):
    for n in order:
        at, rows, cols = WEIGHT_RUNS[n]
        fetch(slots_refs, where_ref, held[n], sems.at[n], base + at, rows, cols)
    return [functools.partial(fetch_done, held[n], sems.at[n]) for n in range(4)]


def first_forward(where_ref, box_ref, x_ref, mods_ref, gathered_ref, passed_ref, middle_ref, out_ref, *rest):
    mask_ref, rest = rest[-1], rest[:-1]
    fill_mask(mask_ref, box_ref, 1)
    mod_ref = mods_ref.at[pl.ds(box_ref[7], 1), 0]
    kept, (wq, wo, w1, w2, sems) = rest[:5], rest[5:]
    weights = (wq, wo, w1, w2)
    waits = fetch_all((gathered_ref, passed_ref), where_ref, weights, sems, 0, (0, 1, 2, 3))
    middle, _, output = forward_part(x_ref[...].astype(f32), mod_ref, mask_ref, weights, waits, kept, None)
    middle_ref[...] = middle
    out_ref[...] = output.astype(bf16)


def second_layer(
    where_ref, place_ref, box_ref, x_ref, up_ref, mods_ref, gathered_ref, passed_ref, out_ref, grad_ref, *rest
):
    mask_ref, rest = rest[-1], rest[:-1]
    fill_mask(mask_ref, box_ref, 4)
    mod_ref = mods_ref.at[:, 1]
    grads_refs, rest = rest[:6], rest[6:]
    kept, (wq, wo, w1, w2, sems, stage, sem, acc, wide_s) = rest[:5], rest[5:]
    weights = (wq, wo, w1, w2)
    waits = fetch_all((gathered_ref, passed_ref), where_ref, weights, sems, LAYER_TILES, (0, 1, 2, 3))
    x = x_ref[...].astype(f32)
    middle, renormed, output = forward_part(x, mod_ref, mask_ref, weights, waits, kept, same_sequence())
    out_ref[...] = output.astype(bf16)
    nothing = [lambda: None] * 4
    grad = backward_part(
        x, middle, renormed, up_ref[...].astype(f32), mod_ref, mask_ref, weights, nothing, kept,
        stage, grads_refs, place_ref.at[pl.ds(LAYER_TILES, LAYER_TILES)], sem, acc, wide_s,
    )
    grad_ref[...] = grad.astype(bf16)
    pltpu.make_async_copy(stage, stage, sem).wait()


def first_backward(
    where_ref, place_ref, box_ref, x_ref, middle_ref, up_ref, mods_ref, gathered_ref, passed_ref,
    qkv_s, probs_s, attended_s, slope_s, active_s, *rest,
):
    mask_ref, rest = rest[-1], rest[:-1]
    fill_mask(mask_ref, box_ref, 1)
    mod_ref = mods_ref.at[pl.ds(box_ref[7], 1), 0]
    grad_ref, *grads_refs = rest[6:13]
    wq, wo, w1, w2, sems, stage, sem, acc, wide_s = rest[13:]
    weights = (wq, wo, w1, w2)
    waits = fetch_all((gathered_ref, passed_ref), where_ref, weights, sems, 0, (3, 2, 1, 0))
    x, middle = x_ref[...].astype(f32), middle_ref[...]
    normal, _inverse = norm_parts(middle)
    renormed = (normal * (1.0 + picked_row(mod_ref, mask_ref, 4)) + picked_row(mod_ref, mask_ref, 3)).astype(bf16)
    grad = backward_part(
        x, middle, renormed, up_ref[...].astype(f32), mod_ref, mask_ref, weights, waits,
        (qkv_s, probs_s, attended_s, slope_s, active_s), stage, grads_refs, place_ref, sem, acc, wide_s,
    )
    grad_ref[...] = grad.astype(bf16)
    pltpu.make_async_copy(stage, stage, sem).wait()


SMEM = pl.BlockSpec(memory_space=pltpu.SMEM)
VMEM = pl.BlockSpec(memory_space=pltpu.VMEM)
ANY = pl.BlockSpec(memory_space=pl.ANY)
MASK = pltpu.VMEM((TOK, BLOCK), f32)
PARAMS = pltpu.CompilerParams(vmem_limit_bytes=60 * 1024 * 1024)
BACK_SCRATCH = [
    pltpu.VMEM((LAYER_TILES, BLOCK, BLOCK), bf16),
    pltpu.SemaphoreType.DMA,
    pltpu.VMEM((TOK, D), f32),
    pltpu.VMEM((9, TOK, CH), bf16),
]


PARTS = (140, 112, 196)
GRADS = [jax.ShapeDtypeStruct((n, BLOCK, BLOCK), bf16) for n in PARTS + PARTS]


def run_first_forward(where, box, x, mods, slots):
    return pl.pallas_call(
        first_forward,
        name="first_forward",
        out_shape=[jax.ShapeDtypeStruct((TOK, D), f32), jax.ShapeDtypeStruct((TOK, D), bf16)]
        + [jax.ShapeDtypeStruct(s, t) for s, t in KEPT],
        in_specs=[SMEM, SMEM, VMEM, VMEM, ANY, ANY],
        out_specs=[VMEM] * 7,
        scratch_shapes=WEIGHT_SCRATCH + [MASK],
        compiler_params=PARAMS,
    )(where, box, x, mods, *slots)


def run_second(where, place, box, x, up, mods, slots):
    return pl.pallas_call(
        second_layer,
        name="second_layer",
        out_shape=[
            jax.ShapeDtypeStruct((TOK, D), bf16),
            jax.ShapeDtypeStruct((TOK, D), bf16),
            *GRADS,
        ],
        in_specs=[SMEM, SMEM, SMEM, VMEM, VMEM, VMEM, ANY, ANY],
        out_specs=[VMEM, VMEM] + [ANY] * 6,
        scratch_shapes=[pltpu.VMEM(s, t) for s, t in KEPT] + WEIGHT_SCRATCH + BACK_SCRATCH + [MASK],
        compiler_params=PARAMS,
    )(where, place, box, x, up, mods, *slots)


def run_first_backward(where, place, box, x, middle, up, mods, slots, kept, grads):
    return pl.pallas_call(
        first_backward,
        name="first_backward",
        out_shape=[
            jax.ShapeDtypeStruct((TOK, D), bf16),
            *GRADS,
        ],
        in_specs=[SMEM] * 3 + [VMEM] * 4 + [ANY] * 2 + [VMEM] * 5 + [ANY] * 6,
        out_specs=[VMEM] + [ANY] * 6,
        scratch_shapes=WEIGHT_SCRATCH + BACK_SCRATCH + [MASK],
        input_output_aliases={14 + k: 1 + k for k in range(6)},
        compiler_params=PARAMS,
    )(where, place, box, x, middle, up, mods, *slots, *kept, *grads)


def everyone():
    for y in range(4):
        for xh in range(2):
            for z in range(4):
                for c in range(2):
                    for xl in range(2):
                        yield (y, xh, z, c, xl)


def number(y, xh, z, c, xl):
    return (((y * 2 + xh) * 4 + z) * 2 + c) * 2 + xl


def permute(value, target):
    return lax.ppermute(value, EVERY, [(number(*d), number(*target(*d))) for d in everyone()])


def along(axis, step):
    def target(y, xh, z, c, xl):
        if (axis == 0) == (c == 0):
            return ((y + step) % 4, xh, z, c, xl)
        return (y, xh, (z + step) % 4, c, xl)

    return target


def other_core(y, xh, z, c, xl):
    return (y, xh, z, 1 - c, xl)


def across(y, xh, z, c, xl):
    return (y, 1 - xh, z, c, 1 - xl)


def twin(y, xh, z, c, xl):
    return (y, xh, z, c, 1 - xl)


def added(*values):
    total = values[0].astype(f32)
    for value in values[1:]:
        total = total + value.astype(f32)
    return total.astype(bf16)


def pair(y, xh, z, c, xl):
    return twin(y, xh, z, c, xl) if c == 0 else across(y, xh, z, c, xl)


def opposite(y, xh, z, c, xl):
    return (y, 1 - xh, z, c, xl)


def pair_last(y, xh, z, c, xl):
    return across(y, xh, z, c, xl) if c == 0 else twin(y, xh, z, c, xl)


PIECES = {
    "plain2": (0, 56), "given2": (56, 28), "given13": (84, 56), "plain13": (140, 112), "kept2": (252, 28),
    "kept13": (280, 56), "given0": (336, 28), "kept0": (364, 28), "plain0": (392, 56),
}
TILE_STEP = 7


def add_tiles(plan, source_count, last_count, *refs):
    sources, outs = refs[:source_count], refs[source_count + last_count :]
    for out, parts in zip(outs, plan):
        for at, size, terms in parts:
            step = TILE_STEP if size % TILE_STEP == 0 else size

            def some(i, carry, out=out, at=at, terms=terms, step=step):
                for k in range(step):
                    n = i * step + k
                    total = sources[terms[0][0]][terms[0][1] + n].astype(f32)
                    for source, start in terms[1:]:
                        total = total + sources[source][start + n].astype(f32)
                    out[at + n] = total.astype(bf16)
                return carry

            lax.fori_loop(0, size // step, some, 0)


def keep(*refs):
    pass


FREE = pl.CostEstimate(flops=1, bytes_accessed=1, transcendentals=0)


class TileSums:
    def __init__(self):
        self.last = []

    def __call__(self, plan, *sources, after=()):
        sizes = [sum(size for _, size, _ in parts) for parts in plan]
        last = [*self.last, *after]
        tiles = sum(sizes) + sum(value.shape[0] for value in sources)
        outs = pl.pallas_call(
            functools.partial(add_tiles, plan, len(sources), len(last)),
            name="add_tiles",
            out_shape=[jax.ShapeDtypeStruct((n, BLOCK, BLOCK), bf16) for n in sizes]
            + [jax.ShapeDtypeStruct((8, BLOCK), f32)],
            in_specs=[VMEM] * (len(sources) + len(self.last)) + [ANY] * len(after),
            out_specs=[VMEM] * (len(sizes) + 1),
            compiler_params=pltpu.CompilerParams(vmem_limit_bytes=tiles * 32768 + 1024 * 1024),
            cost_estimate=FREE,
        )(*sources, *last)
        self.last = [outs[-1]]
        return outs[:-1]


def then(value, *last):
    return pl.pallas_call(
        keep,
        name="keep",
        out_shape=jax.ShapeDtypeStruct(value.shape, value.dtype),
        in_specs=[ANY] * (1 + len(last)),
        out_specs=ANY,
        input_output_aliases={0: 0},
        cost_estimate=FREE,
    )(value, *last)


def reduce_tiles(mine, given, core, frame, token_blocks, send_tokens, renew):
    add = TileSums()
    at = {name: start for name, (start, _) in PIECES.items()}

    def alone(size, *terms):
        return [(0, size, list(terms))]

    got = permute(given[0], other_core)
    p2_a, p2_b, over = add(
        [alone(28, (0, 0), (1, 0)), alone(28, (0, 28), (1, 28)), alone(84, (0, 56), (1, 56))], mine[0], got
    )
    p2_ahead, p2_behind = permute(p2_a, along(0, 1)), permute(p2_b, along(0, -1))
    x213 = permute(over, pair)
    got = permute(then(given[1], *add.last), other_core)
    last_got = permute(then(given[2], *add.last), other_core)
    p13 = add(
        [
            [(0, 28, [(0, 0), (1, 0), (2, 0)]), (28, 28, [(0, 28), (1, 28)])],
            [(0, 28, [(0, 56), (1, 56)]), (28, 28, [(0, 84), (1, 84), (3, 0)])],
        ],
        mine[1], got, p2_ahead, p2_behind,
    )
    p1, p3 = permute(p13[0], along(0, 1)), permute(p13[1], along(0, -1))
    mine, got = mine[2], last_got
    at = {name: start - 252 for name, start in at.items()}
    x0 = permute(add([alone(28, (0, at["given0"]), (1, at["given0"]))], mine, got)[0], pair)
    h2 = add([alone(14, (0, at["kept2"] + n), (1, at["kept2"] + n), (2, n)) for n in (0, 14)], mine, got, x213)
    h2_ahead, h2_behind = permute(h2[0], along(0, 1)), permute(h2[1], along(0, -1))

    def split(start, cuts):
        return [
            alone(size, (0, start + n), (1, start + n), *((k, n) for k in more)) for n, size, more in cuts
        ]

    p = add(
        split(at["plain0"], [(28, 7, (2, 3)), (35, 7, (2, 3)), (0, 14, (2, 3)), (14, 14, (2, 3)), (42, 14, (2, 3))]),
        mine, got, p1, p3,
    )
    ahead, behind = permute(p[0], along(1, 1)), permute(p[1], along(1, -1))
    k13 = r13 = at["kept13"]
    h13 = add(
        [
            [(0, 14, [(0, k13), (1, r13), (2, 28), (3, 0)]), (14, 14, [(0, k13 + 14), (1, r13 + 14), (2, 42)])],
            [(0, 14, [(0, k13 + 28), (1, r13 + 28), (2, 56)]), (14, 14, [(0, k13 + 42), (1, r13 + 42), (2, 70), (4, 0)])],
        ],
        mine, got, x213, h2_ahead, h2_behind,
    )
    h1, h3 = permute(h13[0], along(0, 1)), permute(h13[1], along(0, -1))
    sides = add(
        [
            [(0, 7, [(0, 0), (1, 0)]), (7, 7, [(0, 7)])],
            [(0, 7, [(2, 0)]), (7, 7, [(2, 7), (3, 0)])],
        ],
        p[3], ahead, p[4], behind,
    )
    up, down = permute(sides[0], along(1, 1)), permute(sides[1], along(1, -1))
    h = add(
        split(at["kept0"], [(14, 4, (2, 3, 4)), (18, 3, (2, 3, 4)), (0, 7, (2, 3, 4)), (7, 7, (2, 3, 4)), (21, 7, (2, 3, 4))]),
        mine, got, x0, h1, h3,
    )
    h_ahead, h_behind = permute(h[0], along(1, 1)), permute(h[1], along(1, -1))
    token_blocks = send_tokens(then(token_blocks, *add.last))
    p = add([alone(7, (0, n), (1, n), (2, n)) for n in (0, 7)], p[2], up, down)
    far = permute(p[1], across)
    sides = add(
        [
            [(0, 4, [(0, 0), (1, 0)]), (4, 3, [(0, 4)])],
            [(0, 4, [(2, 0)]), (4, 3, [(2, 4), (3, 0)])],
        ],
        h[3], h_ahead, h[4], h_behind,
    )
    h_up, h_down = permute(sides[0], along(1, 1)), permute(sides[1], along(1, -1))
    (p,) = add([alone(7, (0, 0), (1, 0))], p[0], far)
    match = permute(p, twin)
    (h,) = add([alone(7, (0, 0), (1, 0), (2, 0))], h[2], h_up, h_down, after=[token_blocks])
    beyond, beside, around = permute(h, pair_last), permute(h, twin), permute(h, opposite)
    told = (core == 0) & (frame == 1)
    h = added(jnp.where(told, beside, h), jnp.where(told, around, beyond))
    renewed = renew([p, match])
    return renewed, permute(then(h, renewed[0]), other_core), token_blocks


def precondition(term_count, info_ref, *refs):
    terms, refs = refs[:term_count], refs[term_count:]
    sources, refs = refs[:5], refs[-14:]
    outs, held, made, sems = refs[:4], refs[4:9], refs[9:13], refs[13]
    start = info_ref[0]
    loads = [
        pltpu.make_async_copy(source.at[pl.ds(start, 7)], here, sems.at[n])
        for n, (source, here) in enumerate(zip(sources, held))
    ]
    for load in loads:
        load.start()
    for load in loads:
        load.wait()
    masters, left_stats, right_stats, left_roots, right_roots = held
    grads, new_left, new_right, new_masters = made

    def product(a, b, dims):
        return lax.dot_general(a, b, (dims, ((), ())), preferred_element_type=f32, precision=highest)

    for n in range(7):
        total = terms[0][n].astype(f32)
        for term in terms[1:]:
            total = total + term[n].astype(f32)
        grad = jnp.where(info_ref[1 + start + n] > 0, total, 0.0)
        grads[n] = grad
        new_left[n] = stat_decay * left_stats[n] + (1.0 - stat_decay) * product(grad, grad, ((1,), (1,)))
        new_right[n] = stat_decay * right_stats[n] + (1.0 - stat_decay) * product(grad, grad, ((0,), (0,)))
        rotated = product(grad, right_roots[n], ((1,), (0,)))
        new_masters[n] = masters[n] - learning_rate * product(left_roots[n], rotated, ((1,), (0,)))
    stores = [
        pltpu.make_async_copy(here, out.at[pl.ds(start, 7)], sems.at[n]) for n, (here, out) in enumerate(zip(made, outs))
    ]
    for store in stores:
        store.start()
    for store in stores:
        store.wait()


def run_precondition(info, terms, sources, outs):
    seven = pltpu.VMEM((7, BLOCK, BLOCK), f32)
    return pl.pallas_call(
        functools.partial(precondition, len(terms)),
        name="precondition",
        out_shape=[jax.ShapeDtypeStruct((14, BLOCK, BLOCK), f32)] * 4,
        in_specs=[SMEM] + [VMEM] * len(terms) + [ANY] * (5 + len(outs)),
        out_specs=[ANY] * 4,
        scratch_shapes=[seven] * 9 + [pltpu.SemaphoreType.DMA((5,))],
        input_output_aliases={6 + len(terms) + k: k for k in range(len(outs))},
        compiler_params=pltpu.CompilerParams(vmem_limit_bytes=58 * 1024 * 1024),
        cost_estimate=pl.CostEstimate(flops=7 * 4 * 6 * 2 * BLOCK**3, bytes_accessed=7 * 9 * 65536, transcendentals=0),
    )(info, *terms, *sources, *outs)


BY_GATHER = 7
OTHERS = 14 - BY_GATHER


def gather_tiles(tiles, beside):
    gathered = lax.all_gather(tiles[:BY_GATHER], POS, axis=0, tiled=True)
    here, n = tiles[BY_GATHER:], OTHERS
    base = jnp.concatenate([here, permute(here, across)], axis=0)
    behind, ahead = permute(base, along(1, 1)), permute(base, along(1, -1))
    far = [permute(behind[:n], along(1, 1)), permute(ahead[n:], along(1, -1))]
    own = jnp.concatenate([base, behind, ahead, *far], axis=0)
    behind, ahead = permute(own, along(0, 1)), permute(own, along(0, -1))
    far = [permute(behind[: 4 * n], along(0, 1)), permute(ahead[4 * n :], along(0, -1))]
    near = jnp.concatenate([own, behind, ahead], axis=0)
    far = then(jnp.concatenate(far, axis=0), *beside)
    passed = jnp.concatenate([near, far, permute(near, other_core), permute(far, other_core)], axis=0)
    return gathered, passed


def source_of(slots, y, xh, z, core):
    owner, k = slots // 14, slots % 14
    owner_y, owner_xh, owner_z, owner_c = owner // 16, owner // 8 % 2, owner // 2 % 4, owner % 2
    ahead_y, ahead_z = (owner_y - y) % 4, (owner_z - z) % 4
    first = jnp.where(owner_c == 0, ahead_y, ahead_z)
    second = jnp.where(owner_c == 0, ahead_z, ahead_y)

    def rank(ring):
        return jnp.where(ring == 3, 1, jnp.where(ring == 1, 2, jnp.where(ring == 2, 3, 0)))

    place = (((owner_c + core) % 2 * 4 + rank(first)) * 4 + rank(second)) * 2 + (owner_xh + xh) % 2
    place = 64 * BY_GATHER + place * OTHERS + k - BY_GATHER
    return jnp.where(k < BY_GATHER, owner * BY_GATHER + k, place).astype(jnp.int32)


def place_of(slots, y, xh, z, core, frame):
    owner, k = slots // 14, slots % 14
    owner_y, owner_xh, owner_z, owner_c = owner // 16, owner // 8 % 2, owner // 2 % 4, owner % 2
    handler = k // 7
    ahead_y, ahead_z = (owner_y - y) % 4, (owner_z - z) % 4
    first = jnp.where(handler == 0, ahead_y, ahead_z)
    second = jnp.where(handler == 0, ahead_z, ahead_y)
    over_x = (owner_xh + xh) % 2
    kept = jnp.where(handler == 0, (over_x + frame) % 2, over_x) == 0

    def start(prefix, size):
        at0, at2, at13 = (PIECES[prefix + ring][0] for ring in ("0", "2", "13"))
        return jnp.where(first == 0, at0, jnp.where(first == 2, at2, at13 + size * (first // 2)))

    plain = start("plain", 56) + (second * 2 + over_x) * 7
    halved = jnp.where(kept, start("kept", 28), start("given", 28)) + second * 7
    place = jnp.where(owner_c == handler, plain, halved) + k % 7
    return ((handler + core) % 2 * 448 + place).astype(jnp.int32)


def local(
    tokens,
    modulation,
    box_bounds,
    masters,
    left_stats,
    right_stats,
    left_roots,
    right_roots,
    owner_slot,
    cotangent,
):
    y, xh, z, core = (lax.axis_index(a) for a in POS)
    mine, copy = lax.axis_index(POS), lax.axis_index("frame")

    def to_frames(value):
        return lax.all_to_all(value.reshape(64, 4, D), POS, 0, 0, tiled=True).reshape(TOK, D)

    clip, frame = mine // 16, mine % 16
    bounds_here = lax.dynamic_index_in_dim(box_bounds, clip, 0, keepdims=False)
    box_first = jnp.concatenate([bounds_here, jnp.stack([frame, clip])]).astype(jnp.int32)
    box_second = jnp.concatenate([box_bounds.reshape(24), jnp.stack([mine * 4])]).astype(jnp.int32)
    where = source_of(owner_slot, y, xh, z, core)
    place = place_of(owner_slot, y, xh, z, core, copy)
    upstream = cotangent.reshape(TOK, D)
    tokens_here = to_frames(tokens)
    slots = gather_tiles(masters.astype(bf16), [tokens_here, where, place])
    middle, passed, *kept = run_first_forward(where, box_first, tokens_here, modulation, slots)
    here = to_frames(passed)
    block_output, grad_here, *grads = run_second(where, place, box_second, here, upstream, modulation, slots)
    upstream = to_frames(grad_here)
    token_grads, *grads = run_first_backward(
        where, place, box_first, tokens_here, middle, upstream, modulation, slots, kept, grads
    )
    slot_ids = mine * 14 + jnp.arange(14, dtype=jnp.int32)
    holds = jnp.any(owner_slot[None, :] == slot_ids[:, None], axis=1)
    sources = [masters, left_stats, right_stats, left_roots, right_roots]

    def info(start):
        return jnp.concatenate([jnp.stack([start]), holds]).astype(jnp.int32)

    def renew(terms):
        return run_precondition(info(core * 7), terms, sources, [])

    renewed, halved, token_grads = reduce_tiles(grads[:3], grads[3:], core, copy, token_grads, to_frames, renew)
    renewed = run_precondition(info(7 - core * 7), [halved], sources, renewed)
    return (block_output.reshape(tokens.shape), token_grads.reshape(tokens.shape), *renewed)


def solution(mesh):
    split = Mesh(
        mesh.devices.reshape(4, 2, 4, 2, mesh.shape["frame"]),
        ("pos_0", "pos_1", "pos_2", "pos_3", "frame"),
    )
    return jax.shard_map(
        local,
        mesh=split,
        in_specs=(
            P("frame", None, POS, None),
            P("frame", None, None, None, None),
            P("frame", None),
            P(POS, None, None),
            P(POS, None, None),
            P(POS, None, None),
            P(POS, None, None),
            P(POS, None, None),
            P(),
            P("frame", None, POS, None),
        ),
        out_specs=(
            P("frame", None, POS, None),
            P("frame", None, POS, None),
            P(POS, None, None),
            P(POS, None, None),
            P(POS, None, None),
            P(POS, None, None),
        ),
        check_vma=False,
    )
```

```python
import functools

import jax
import jax.numpy as jnp
from jax import lax
from jax.experimental import pallas as pl
from jax.experimental.pallas import tpu as pltpu
from jax.sharding import Mesh
from jax.sharding import PartitionSpec as P

D = 768
HEADS = 12
HD = 64
FF = 3072
GRID = 16
BLOCK = 128
TOK = 256
CH = 256
POS = ("pos_0", "pos_1", "pos_2", "pos_3")
EVERY = ("pos_0", "pos_1", "pos_2", "pos_3", "frame")

highest = lax.Precision.HIGHEST
stat_decay = 0.5
learning_rate = 0.7
norm_epsilon = 1e-06
f32 = jnp.float32
bf16 = jnp.bfloat16

QKV_AT, OUT_AT, FIRST_AT, SECOND_AT, LAYER_TILES = 0, 108, 144, 288, 432


def dot_nn(a, b):
    return lax.dot_general(a, b, (((1,), (0,)), ((), ())), preferred_element_type=f32)


def dot_nt(a, b):
    return lax.dot_general(a, b, (((1,), (1,)), ((), ())), preferred_element_type=f32)


def dot_tn(a, b):
    return lax.dot_general(a, b, (((0,), (0,)), ((), ())), preferred_element_type=f32)


def side(parts):
    return jnp.concatenate(parts, axis=1)


def norm_parts(values):
    center = values - jnp.mean(values, axis=-1, keepdims=True)
    spread = jnp.mean(center * center, axis=-1, keepdims=True)
    inverse = lax.rsqrt(spread + norm_epsilon)
    return center * inverse, inverse


def norm_back(normal, inverse, grad):
    return inverse * (
        grad
        - jnp.mean(grad, axis=-1, keepdims=True)
        - normal * jnp.mean(grad * normal, axis=-1, keepdims=True)
    )


def fill_mask(mask_ref, box_ref, clips):
    span = TOK // clips
    ids = lax.broadcasted_iota(jnp.int32, (span, BLOCK), 0)
    for clip in range(clips):
        low_f, high_f, low_r, high_r, low_c, high_c = (box_ref[6 * clip + k] for k in range(6))
        base = box_ref[6 * clips]
        frames = jnp.full((span, BLOCK), base, jnp.int32) if clips == 1 else ids >> 2
        patches = ids if clips == 1 else base + (ids & 3)
        rows, cols = patches >> 4, patches & 15
        within = (low_f <= frames) & (frames < high_f) & (low_r <= rows) & (rows < high_r) & (low_c <= cols) & (cols < high_c)
        mask_ref[clip * span : (clip + 1) * span, :] = jnp.where(within, 1.0, 0.0)


def picked_row(mod_ref, mask_ref, row):
    clips = mod_ref.shape[0]
    span = TOK // clips
    parts = []
    for clip in range(clips):
        inside_box = side([mask_ref[clip * span : (clip + 1) * span, :]] * (D // BLOCK)) > 0.5
        parts.append(
            jnp.where(
                inside_box,
                jnp.broadcast_to(mod_ref[clip, 1, row : row + 1, :], (span, D)),
                jnp.broadcast_to(mod_ref[clip, 0, row : row + 1, :], (span, D)),
            )
        )
    return parts[0] if clips == 1 else jnp.concatenate(parts, axis=0)


def fetch(slots_refs, where_ref, held, sem, base, row_tiles, col_tiles):
    step = 6

    def one(turn, carry):
        col = turn // (row_tiles // step)
        first = (turn % (row_tiles // step)) * step
        for k in range(step):
            row = first + k
            target = held.at[col, pl.ds(pl.multiple_of(row * BLOCK, BLOCK), BLOCK), :]
            place = where_ref[base + row * col_tiles + col]
            for ref, start, end in ((slots_refs[0], 0, 64 * BY_GATHER), (slots_refs[1], 64 * BY_GATHER, 64 * 14)):

                @pl.when(jnp.logical_and(place >= start, place < end))
                def _(ref=ref, start=start):
                    pltpu.make_async_copy(ref.at[place - start], target, sem).start()

        return carry

    lax.fori_loop(0, col_tiles * (row_tiles // step), one, 0)


def fetch_done(held, sem):
    pltpu.make_async_copy(held, held, sem).wait()


def forward_part(x, mod_ref, mask_ref, weights, waits, kept, same):
    wq, wo, w1, w2 = weights
    qkv_s, probs_s, attended_s, slope_s, active_s = kept
    lane = lax.broadcasted_iota(jnp.int32, (TOK, BLOCK), 1)
    low_half = lane < HD

    normal, _ = norm_parts(x)
    normed = (normal * (1.0 + picked_row(mod_ref, mask_ref, 1)) + picked_row(mod_ref, mask_ref, 0)).astype(bf16)
    waits[0]()

    def project(j, carry):
        qkv_s[j] = dot_nn(normed, side([wq[2 * j], wq[2 * j + 1]])).astype(bf16)
        return carry

    lax.fori_loop(0, 9, project, 0, unroll=True)

    def attend(c, carry):
        for pair in range(2):
            cols = slice(pair * BLOCK, (pair + 1) * BLOCK)
            q, k, v = qkv_s[c, :, cols], qkv_s[3 + c, :, cols], qkv_s[6 + c, :, cols]
            outs = []
            for e in range(2):
                mine = low_half if e == 0 else jnp.logical_not(low_half)
                scores = dot_nt(k, jnp.where(mine, q, jnp.zeros_like(q))) * HD ** (-0.5)
                if same is not None:
                    scores = jnp.where(same, scores, -jnp.inf)
                grown = jnp.exp(scores - jnp.max(scores, axis=0, keepdims=True))
                probs = (grown * (1.0 / jnp.sum(grown, axis=0, keepdims=True))).astype(bf16)
                probs_s[4 * c + 2 * pair + e] = probs
                outs.append(dot_tn(probs, v))
            attended_s[c, :, cols] = jnp.where(low_half, outs[0], outs[1]).astype(bf16)
        return carry

    lax.fori_loop(0, 3, attend, 0, unroll=True)
    attended = side([attended_s[c] for c in range(3)])
    waits[1]()
    branch = side([dot_nn(attended, side([wo[2 * j], wo[2 * j + 1]])) for j in range(3)])
    middle = x + picked_row(mod_ref, mask_ref, 2) * branch
    normal, _ = norm_parts(middle)
    renormed = (normal * (1.0 + picked_row(mod_ref, mask_ref, 4)) + picked_row(mod_ref, mask_ref, 3)).astype(bf16)
    waits[2]()

    def widen(j, carry):
        u = dot_nn(renormed, side([w1[2 * j], w1[2 * j + 1]]))
        root = (2.0 / 3.141592653589793) ** 0.5
        square = u * u
        bent = jnp.tanh(root * (u + 0.044715 * (square * u)))
        active_s[j] = (0.5 * u * (1.0 + bent)).astype(bf16)
        slope_s[j] = (
            0.5 * (1.0 + bent) + 0.5 * u * (1.0 - bent * bent) * (root * (1.0 + 3 * 0.044715 * square))
        ).astype(bf16)
        return carry

    lax.fori_loop(0, 12, widen, 0, unroll=True)
    active = side([active_s[j] for j in range(12)])
    waits[3]()
    mlp = side([dot_nn(active, side([w2[2 * j], w2[2 * j + 1]])) for j in range(3)])
    return middle, renormed, middle + picked_row(mod_ref, mask_ref, 5) * mlp


def send_tile(tile_ref, place, grads_refs, sem):
    start = 0
    for ref in grads_refs:
        size = ref.shape[0]

        @pl.when(jnp.logical_and(place >= start, place < start + size))
        def _(ref=ref, start=start):
            pltpu.make_async_copy(tile_ref, ref.at[place - start], sem).start()

        start += size


def send_tiles(stage, grads_refs, place_ref, sem, at, col_tiles, value, row, col):
    rows, cols = value.shape[0] // BLOCK, value.shape[1] // BLOCK
    for j in range(cols):
        for i in range(rows):
            tile = at + (row + i) * col_tiles + (col + j)
            stage[tile] = value[i * BLOCK : (i + 1) * BLOCK, j * BLOCK : (j + 1) * BLOCK].astype(bf16)
            send_tile(stage.at[tile], place_ref[tile], grads_refs, sem)


def backward_part(x, middle, renormed, upstream, mod_ref, mask_ref, weights, waits, kept, stage, grads_refs, place_ref, sem, acc, wide_s):
    wq, wo, w1, w2 = weights
    qkv_s, probs_s, attended_s, slope_s, active_s = kept
    lane = lax.broadcasted_iota(jnp.int32, (TOK, BLOCK), 1)
    low_half = lane < HD
    send = functools.partial(send_tiles, stage, grads_refs, place_ref, sem)

    grad_mlp = (picked_row(mod_ref, mask_ref, 5) * upstream).astype(bf16)
    renormed_t = renormed.T
    acc[...] = jnp.zeros_like(acc)
    waits[3]()
    waits[2]()

    def narrow(j, carry):
        rows = pl.ds(pl.multiple_of(j * CH, CH), CH)
        grad_active = dot_nt(grad_mlp, side([w2[n, rows, :] for n in range(6)]))
        grad_hidden = (grad_active * slope_s[j].astype(f32)).astype(bf16)
        acc[...] += dot_nt(grad_hidden, side([w1[2 * j], w1[2 * j + 1]]))
        send(FIRST_AT, 24, dot_nn(renormed_t, grad_hidden), 0, 2 * j)
        send(SECOND_AT, 6, dot_tn(active_s[j], grad_mlp), 2 * j, 0)
        return carry

    lax.fori_loop(0, 12, narrow, 0, unroll=True)
    normal, inverse = norm_parts(middle)
    grad_middle = upstream + norm_back(normal, inverse, (1.0 + picked_row(mod_ref, mask_ref, 4)) * acc[...])
    grad_branch = (picked_row(mod_ref, mask_ref, 2) * grad_middle).astype(bf16)
    waits[1]()

    def attend(c, carry):
        rows = pl.ds(pl.multiple_of(c * CH, CH), CH)
        grad_attended = dot_nt(grad_branch, side([wo[n, rows, :] for n in range(6)])).astype(bf16)
        send(OUT_AT, 6, dot_tn(attended_s[c], grad_branch), 2 * c, 0)
        for pair in range(2):
            cols = slice(pair * BLOCK, (pair + 1) * BLOCK)
            q, k, v = qkv_s[c, :, cols], qkv_s[3 + c, :, cols], qkv_s[6 + c, :, cols]
            ga = grad_attended[:, cols]
            grads = []
            for e in range(2):
                mine = low_half if e == 0 else jnp.logical_not(low_half)
                probs_low = probs_s[4 * c + 2 * pair + e]
                probs = probs_low.astype(f32)
                weighed = probs * dot_nt(v, jnp.where(mine, ga, jnp.zeros_like(ga)))
                grad_scores = (weighed - probs * jnp.sum(weighed, axis=0, keepdims=True)).astype(bf16)
                grads.append((dot_tn(grad_scores, k), dot_nn(grad_scores, q), dot_nn(probs_low, ga)))
            for n, scaling in ((0, HD ** (-0.5)), (1, HD ** (-0.5)), (2, 1.0)):
                wide_s[3 * n + c, :, cols] = (
                    jnp.where(low_half, grads[0][n], grads[1][n]) * scaling
                ).astype(bf16)
        return carry

    lax.fori_loop(0, 3, attend, 0, unroll=True)
    normal, inverse = norm_parts(x)
    scale_one = 1.0 + picked_row(mod_ref, mask_ref, 1)
    normed_t = (normal * scale_one + picked_row(mod_ref, mask_ref, 0)).astype(bf16).T
    acc[...] = jnp.zeros_like(acc)
    waits[0]()

    def gather_in(j, carry):
        piece = wide_s[j]
        acc[...] += dot_nt(piece, side([wq[2 * j], wq[2 * j + 1]]))
        send(QKV_AT, 18, dot_nn(normed_t, piece), 0, 2 * j)
        return carry

    lax.fori_loop(0, 9, gather_in, 0, unroll=True)
    normal, inverse = norm_parts(x)
    return grad_middle + norm_back(normal, inverse, scale_one * acc[...])


def same_sequence():
    rows = lax.broadcasted_iota(jnp.int32, (TOK, TOK), 0)
    cols = lax.broadcasted_iota(jnp.int32, (TOK, TOK), 1)
    return jnp.logical_and(rows // 64 == cols // 64, rows % 4 == cols % 4)


WEIGHT_SCRATCH = [
    pltpu.VMEM((18, D, BLOCK), bf16),
    pltpu.VMEM((6, D, BLOCK), bf16),
    pltpu.VMEM((24, D, BLOCK), bf16),
    pltpu.VMEM((6, FF, BLOCK), bf16),
    pltpu.SemaphoreType.DMA((4,)),
]
KEPT = [
    ((9, TOK, CH), bf16),
    ((HEADS, TOK, TOK), bf16),
    ((3, TOK, CH), bf16),
    ((12, TOK, CH), bf16),
    ((12, TOK, CH), bf16),
]
WEIGHT_RUNS = ((QKV_AT, 6, 18), (OUT_AT, 6, 6), (FIRST_AT, 6, 24), (SECOND_AT, 24, 6))


def fetch_all(slots_refs, where_ref, held, sems, base, order):
    for n in order:
        at, rows, cols = WEIGHT_RUNS[n]
        fetch(slots_refs, where_ref, held[n], sems.at[n], base + at, rows, cols)
    return [functools.partial(fetch_done, held[n], sems.at[n]) for n in range(4)]


def first_forward(where_ref, box_ref, x_ref, mods_ref, gathered_ref, passed_ref, middle_ref, out_ref, *rest):
    mask_ref, rest = rest[-1], rest[:-1]
    fill_mask(mask_ref, box_ref, 1)
    mod_ref = mods_ref.at[pl.ds(box_ref[7], 1), 0]
    kept, (wq, wo, w1, w2, sems) = rest[:5], rest[5:]
    weights = (wq, wo, w1, w2)
    waits = fetch_all((gathered_ref, passed_ref), where_ref, weights, sems, 0, (0, 1, 2, 3))
    middle, _, output = forward_part(x_ref[...].astype(f32), mod_ref, mask_ref, weights, waits, kept, None)
    middle_ref[...] = middle
    out_ref[...] = output.astype(bf16)


def second_layer(
    where_ref, place_ref, box_ref, x_ref, up_ref, mods_ref, gathered_ref, passed_ref, out_ref, grad_ref, *rest
):
    mask_ref, rest = rest[-1], rest[:-1]
    fill_mask(mask_ref, box_ref, 4)
    mod_ref = mods_ref.at[:, 1]
    grads_refs, rest = rest[:6], rest[6:]
    kept, (wq, wo, w1, w2, sems, stage, sem, acc, wide_s) = rest[:5], rest[5:]
    weights = (wq, wo, w1, w2)
    waits = fetch_all((gathered_ref, passed_ref), where_ref, weights, sems, LAYER_TILES, (0, 1, 2, 3))
    x = x_ref[...].astype(f32)
    middle, renormed, output = forward_part(x, mod_ref, mask_ref, weights, waits, kept, same_sequence())
    out_ref[...] = output.astype(bf16)
    nothing = [lambda: None] * 4
    grad = backward_part(
        x, middle, renormed, up_ref[...].astype(f32), mod_ref, mask_ref, weights, nothing, kept,
        stage, grads_refs, place_ref.at[pl.ds(LAYER_TILES, LAYER_TILES)], sem, acc, wide_s,
    )
    grad_ref[...] = grad.astype(bf16)
    pltpu.make_async_copy(stage, stage, sem).wait()


def first_backward(
    where_ref, place_ref, box_ref, x_ref, middle_ref, up_ref, mods_ref, gathered_ref, passed_ref,
    qkv_s, probs_s, attended_s, slope_s, active_s, *rest,
):
    mask_ref, rest = rest[-1], rest[:-1]
    fill_mask(mask_ref, box_ref, 1)
    mod_ref = mods_ref.at[pl.ds(box_ref[7], 1), 0]
    grad_ref, *grads_refs = rest[6:13]
    wq, wo, w1, w2, sems, stage, sem, acc, wide_s = rest[13:]
    weights = (wq, wo, w1, w2)
    waits = fetch_all((gathered_ref, passed_ref), where_ref, weights, sems, 0, (3, 2, 1, 0))
    x, middle = x_ref[...].astype(f32), middle_ref[...]
    normal, _inverse = norm_parts(middle)
    renormed = (normal * (1.0 + picked_row(mod_ref, mask_ref, 4)) + picked_row(mod_ref, mask_ref, 3)).astype(bf16)
    grad = backward_part(
        x, middle, renormed, up_ref[...].astype(f32), mod_ref, mask_ref, weights, waits,
        (qkv_s, probs_s, attended_s, slope_s, active_s), stage, grads_refs, place_ref, sem, acc, wide_s,
    )
    grad_ref[...] = grad.astype(bf16)
    pltpu.make_async_copy(stage, stage, sem).wait()


SMEM = pl.BlockSpec(memory_space=pltpu.SMEM)
VMEM = pl.BlockSpec(memory_space=pltpu.VMEM)
ANY = pl.BlockSpec(memory_space=pl.ANY)
MASK = pltpu.VMEM((TOK, BLOCK), f32)
PARAMS = pltpu.CompilerParams(vmem_limit_bytes=60 * 1024 * 1024)
BACK_SCRATCH = [
    pltpu.VMEM((LAYER_TILES, BLOCK, BLOCK), bf16),
    pltpu.SemaphoreType.DMA,
    pltpu.VMEM((TOK, D), f32),
    pltpu.VMEM((9, TOK, CH), bf16),
]


PARTS = (140, 112, 196)
GRADS = [jax.ShapeDtypeStruct((n, BLOCK, BLOCK), bf16) for n in PARTS + PARTS]


def run_first_forward(where, box, x, mods, slots):
    return pl.pallas_call(
        first_forward,
        name="first_forward",
        out_shape=[jax.ShapeDtypeStruct((TOK, D), f32), jax.ShapeDtypeStruct((TOK, D), bf16)]
        + [jax.ShapeDtypeStruct(s, t) for s, t in KEPT],
        in_specs=[SMEM, SMEM, VMEM, VMEM, ANY, ANY],
        out_specs=[VMEM] * 7,
        scratch_shapes=WEIGHT_SCRATCH + [MASK],
        compiler_params=PARAMS,
    )(where, box, x, mods, *slots)


def run_second(where, place, box, x, up, mods, slots):
    return pl.pallas_call(
        second_layer,
        name="second_layer",
        out_shape=[
            jax.ShapeDtypeStruct((TOK, D), bf16),
            jax.ShapeDtypeStruct((TOK, D), bf16),
            *GRADS,
        ],
        in_specs=[SMEM, SMEM, SMEM, VMEM, VMEM, VMEM, ANY, ANY],
        out_specs=[VMEM, VMEM] + [ANY] * 6,
        scratch_shapes=[pltpu.VMEM(s, t) for s, t in KEPT] + WEIGHT_SCRATCH + BACK_SCRATCH + [MASK],
        compiler_params=PARAMS,
    )(where, place, box, x, up, mods, *slots)


def run_first_backward(where, place, box, x, middle, up, mods, slots, kept, grads):
    return pl.pallas_call(
        first_backward,
        name="first_backward",
        out_shape=[
            jax.ShapeDtypeStruct((TOK, D), bf16),
            *GRADS,
        ],
        in_specs=[SMEM] * 3 + [VMEM] * 4 + [ANY] * 2 + [VMEM] * 5 + [ANY] * 6,
        out_specs=[VMEM] + [ANY] * 6,
        scratch_shapes=WEIGHT_SCRATCH + BACK_SCRATCH + [MASK],
        input_output_aliases={14 + k: 1 + k for k in range(6)},
        compiler_params=PARAMS,
    )(where, place, box, x, middle, up, mods, *slots, *kept, *grads)


def everyone():
    for y in range(4):
        for xh in range(2):
            for z in range(4):
                for c in range(2):
                    for xl in range(2):
                        yield (y, xh, z, c, xl)


def number(y, xh, z, c, xl):
    return (((y * 2 + xh) * 4 + z) * 2 + c) * 2 + xl


def permute(value, target):
    return lax.ppermute(value, EVERY, [(number(*d), number(*target(*d))) for d in everyone()])


def along(axis, step):
    def target(y, xh, z, c, xl):
        if (axis == 0) == (c == 0):
            return ((y + step) % 4, xh, z, c, xl)
        return (y, xh, (z + step) % 4, c, xl)

    return target


def other_core(y, xh, z, c, xl):
    return (y, xh, z, 1 - c, xl)


def across(y, xh, z, c, xl):
    return (y, 1 - xh, z, c, 1 - xl)


def twin(y, xh, z, c, xl):
    return (y, xh, z, c, 1 - xl)


def added(*values):
    total = values[0].astype(f32)
    for value in values[1:]:
        total = total + value.astype(f32)
    return total.astype(bf16)


def pair(y, xh, z, c, xl):
    return twin(y, xh, z, c, xl) if c == 0 else across(y, xh, z, c, xl)


def opposite(y, xh, z, c, xl):
    return (y, 1 - xh, z, c, xl)


def pair_last(y, xh, z, c, xl):
    return across(y, xh, z, c, xl) if c == 0 else twin(y, xh, z, c, xl)


PIECES = {
    "plain2": (0, 56), "given2": (56, 28), "given13": (84, 56), "plain13": (140, 112), "kept2": (252, 28),
    "kept13": (280, 56), "given0": (336, 28), "kept0": (364, 28), "plain0": (392, 56),
}
TILE_STEP = 7


def add_tiles(plan, source_count, last_count, *refs):
    sources, outs = refs[:source_count], refs[source_count + last_count :]
    for out, parts in zip(outs, plan):
        for at, size, terms in parts:
            step = TILE_STEP if size % TILE_STEP == 0 else size

            def some(i, carry, out=out, at=at, terms=terms, step=step):
                for k in range(step):
                    n = i * step + k
                    total = sources[terms[0][0]][terms[0][1] + n].astype(f32)
                    for source, start in terms[1:]:
                        total = total + sources[source][start + n].astype(f32)
                    out[at + n] = total.astype(bf16)
                return carry

            lax.fori_loop(0, size // step, some, 0)


def keep(*refs):
    pass


FREE = pl.CostEstimate(flops=1, bytes_accessed=1, transcendentals=0)


class TileSums:
    def __init__(self):
        self.last = []

    def __call__(self, plan, *sources, after=()):
        sizes = [sum(size for _, size, _ in parts) for parts in plan]
        last = [*self.last, *after]
        tiles = sum(sizes) + sum(value.shape[0] for value in sources)
        outs = pl.pallas_call(
            functools.partial(add_tiles, plan, len(sources), len(last)),
            name="add_tiles",
            out_shape=[jax.ShapeDtypeStruct((n, BLOCK, BLOCK), bf16) for n in sizes]
            + [jax.ShapeDtypeStruct((8, BLOCK), f32)],
            in_specs=[VMEM] * (len(sources) + len(self.last)) + [ANY] * len(after),
            out_specs=[VMEM] * (len(sizes) + 1),
            compiler_params=pltpu.CompilerParams(vmem_limit_bytes=tiles * 32768 + 1024 * 1024),
            cost_estimate=FREE,
        )(*sources, *last)
        self.last = [outs[-1]]
        return outs[:-1]


def then(value, *last):
    return pl.pallas_call(
        keep,
        name="keep",
        out_shape=jax.ShapeDtypeStruct(value.shape, value.dtype),
        in_specs=[ANY] * (1 + len(last)),
        out_specs=ANY,
        input_output_aliases={0: 0},
        cost_estimate=FREE,
    )(value, *last)


def reduce_tiles(mine, given, core, frame, token_blocks, send_tokens, renew):
    add = TileSums()
    at = {name: start for name, (start, _) in PIECES.items()}

    def alone(size, *terms):
        return [(0, size, list(terms))]

    got = permute(given[0], other_core)
    p2_a, p2_b, over = add(
        [alone(28, (0, 0), (1, 0)), alone(28, (0, 28), (1, 28)), alone(84, (0, 56), (1, 56))], mine[0], got
    )
    p2_ahead, p2_behind = permute(p2_a, along(0, 1)), permute(p2_b, along(0, -1))
    x213 = permute(over, pair)
    got = permute(then(given[1], *add.last), other_core)
    last_got = permute(then(given[2], *add.last), other_core)
    p13 = add(
        [
            [(0, 28, [(0, 0), (1, 0), (2, 0)]), (28, 28, [(0, 28), (1, 28)])],
            [(0, 28, [(0, 56), (1, 56)]), (28, 28, [(0, 84), (1, 84), (3, 0)])],
        ],
        mine[1], got, p2_ahead, p2_behind,
    )
    p1, p3 = permute(p13[0], along(0, 1)), permute(p13[1], along(0, -1))
    mine, got = mine[2], last_got
    at = {name: start - 252 for name, start in at.items()}
    x0 = permute(add([alone(28, (0, at["given0"]), (1, at["given0"]))], mine, got)[0], pair)
    h2 = add([alone(14, (0, at["kept2"] + n), (1, at["kept2"] + n), (2, n)) for n in (0, 14)], mine, got, x213)
    h2_ahead, h2_behind = permute(h2[0], along(0, 1)), permute(h2[1], along(0, -1))

    def split(start, cuts):
        return [
            alone(size, (0, start + n), (1, start + n), *((k, n) for k in more)) for n, size, more in cuts
        ]

    p = add(
        split(at["plain0"], [(28, 7, (2, 3)), (35, 7, (2, 3)), (0, 14, (2, 3)), (14, 14, (2, 3)), (42, 14, (2, 3))]),
        mine, got, p1, p3,
    )
    ahead, behind = permute(p[0], along(1, 1)), permute(p[1], along(1, -1))
    k13 = r13 = at["kept13"]
    h13 = add(
        [
            [(0, 14, [(0, k13), (1, r13), (2, 28), (3, 0)]), (14, 14, [(0, k13 + 14), (1, r13 + 14), (2, 42)])],
            [(0, 14, [(0, k13 + 28), (1, r13 + 28), (2, 56)]), (14, 14, [(0, k13 + 42), (1, r13 + 42), (2, 70), (4, 0)])],
        ],
        mine, got, x213, h2_ahead, h2_behind,
    )
    h1, h3 = permute(h13[0], along(0, 1)), permute(h13[1], along(0, -1))
    sides = add(
        [
            [(0, 7, [(0, 0), (1, 0)]), (7, 7, [(0, 7)])],
            [(0, 7, [(2, 0)]), (7, 7, [(2, 7), (3, 0)])],
        ],
        p[3], ahead, p[4], behind,
    )
    up, down = permute(sides[0], along(1, 1)), permute(sides[1], along(1, -1))
    h = add(
        split(at["kept0"], [(14, 4, (2, 3, 4)), (18, 3, (2, 3, 4)), (0, 7, (2, 3, 4)), (7, 7, (2, 3, 4)), (21, 7, (2, 3, 4))]),
        mine, got, x0, h1, h3,
    )
    h_ahead, h_behind = permute(h[0], along(1, 1)), permute(h[1], along(1, -1))
    p = add([alone(7, (0, n), (1, n), (2, n)) for n in (0, 7)], p[2], up, down)
    far = permute(p[1], across)
    sides = add(
        [
            [(0, 4, [(0, 0), (1, 0)]), (4, 3, [(0, 4)])],
            [(0, 4, [(2, 0)]), (4, 3, [(2, 4), (3, 0)])],
        ],
        h[3], h_ahead, h[4], h_behind,
    )
    h_up, h_down = permute(sides[0], along(1, 1)), permute(sides[1], along(1, -1))
    (p,) = add([alone(7, (0, 0), (1, 0))], p[0], far)
    match = permute(p, twin)
    (h,) = add([alone(7, (0, 0), (1, 0), (2, 0))], h[2], h_up, h_down)
    token_blocks = send_tokens(then(token_blocks, *add.last))
    beyond, beside, around = permute(h, pair_last), permute(h, twin), permute(h, opposite)
    told = (core == 0) & (frame == 1)
    h = added(jnp.where(told, beside, h), jnp.where(told, around, beyond))
    renewed = renew([p, match])
    return renewed, permute(then(h, renewed[0]), other_core), token_blocks


def precondition(term_count, info_ref, *refs):
    terms, refs = refs[:term_count], refs[term_count:]
    sources, refs = refs[:5], refs[-14:]
    outs, held, made, sems = refs[:4], refs[4:9], refs[9:13], refs[13]
    start = info_ref[0]
    loads = [
        pltpu.make_async_copy(source.at[pl.ds(start, 7)], here, sems.at[n])
        for n, (source, here) in enumerate(zip(sources, held))
    ]
    for load in loads:
        load.start()
    for load in loads:
        load.wait()
    masters, left_stats, right_stats, left_roots, right_roots = held
    grads, new_left, new_right, new_masters = made

    def product(a, b, dims):
        return lax.dot_general(a, b, (dims, ((), ())), preferred_element_type=f32, precision=highest)

    for n in range(7):
        total = terms[0][n].astype(f32)
        for term in terms[1:]:
            total = total + term[n].astype(f32)
        grad = jnp.where(info_ref[1 + start + n] > 0, total, 0.0)
        grads[n] = grad
        new_left[n] = stat_decay * left_stats[n] + (1.0 - stat_decay) * product(grad, grad, ((1,), (1,)))
        new_right[n] = stat_decay * right_stats[n] + (1.0 - stat_decay) * product(grad, grad, ((0,), (0,)))
        rotated = product(grad, right_roots[n], ((1,), (0,)))
        new_masters[n] = masters[n] - learning_rate * product(left_roots[n], rotated, ((1,), (0,)))
    stores = [
        pltpu.make_async_copy(here, out.at[pl.ds(start, 7)], sems.at[n]) for n, (here, out) in enumerate(zip(made, outs))
    ]
    for store in stores:
        store.start()
    for store in stores:
        store.wait()


def run_precondition(info, terms, sources, outs):
    seven = pltpu.VMEM((7, BLOCK, BLOCK), f32)
    return pl.pallas_call(
        functools.partial(precondition, len(terms)),
        name="precondition",
        out_shape=[jax.ShapeDtypeStruct((14, BLOCK, BLOCK), f32)] * 4,
        in_specs=[SMEM] + [VMEM] * len(terms) + [ANY] * (5 + len(outs)),
        out_specs=[ANY] * 4,
        scratch_shapes=[seven] * 9 + [pltpu.SemaphoreType.DMA((5,))],
        input_output_aliases={6 + len(terms) + k: k for k in range(len(outs))},
        compiler_params=pltpu.CompilerParams(vmem_limit_bytes=58 * 1024 * 1024),
        cost_estimate=pl.CostEstimate(flops=7 * 4 * 6 * 2 * BLOCK**3, bytes_accessed=7 * 9 * 65536, transcendentals=0),
    )(info, *terms, *sources, *outs)


BY_GATHER = 7
OTHERS = 14 - BY_GATHER


def gather_tiles(tiles, beside):
    gathered = lax.all_gather(tiles[:BY_GATHER], POS, axis=0, tiled=True)
    here, n = tiles[BY_GATHER:], OTHERS
    base = jnp.concatenate([here, permute(here, across)], axis=0)
    behind, ahead = permute(base, along(1, 1)), permute(base, along(1, -1))
    far = [permute(behind[:n], along(1, 1)), permute(ahead[n:], along(1, -1))]
    own = jnp.concatenate([base, behind, ahead, *far], axis=0)
    behind, ahead = permute(own, along(0, 1)), permute(own, along(0, -1))
    far = [permute(behind[: 4 * n], along(0, 1)), permute(ahead[4 * n :], along(0, -1))]
    near = jnp.concatenate([own, behind, ahead], axis=0)
    far = then(jnp.concatenate(far, axis=0), *beside)
    passed = jnp.concatenate([near, far, permute(near, other_core), permute(far, other_core)], axis=0)
    return gathered, passed


def source_of(slots, y, xh, z, core):
    owner, k = slots // 14, slots % 14
    owner_y, owner_xh, owner_z, owner_c = owner // 16, owner // 8 % 2, owner // 2 % 4, owner % 2
    ahead_y, ahead_z = (owner_y - y) % 4, (owner_z - z) % 4
    first = jnp.where(owner_c == 0, ahead_y, ahead_z)
    second = jnp.where(owner_c == 0, ahead_z, ahead_y)

    def rank(ring):
        return jnp.where(ring == 3, 1, jnp.where(ring == 1, 2, jnp.where(ring == 2, 3, 0)))

    place = (((owner_c + core) % 2 * 4 + rank(first)) * 4 + rank(second)) * 2 + (owner_xh + xh) % 2
    place = 64 * BY_GATHER + place * OTHERS + k - BY_GATHER
    return jnp.where(k < BY_GATHER, owner * BY_GATHER + k, place).astype(jnp.int32)


def place_of(slots, y, xh, z, core, frame):
    owner, k = slots // 14, slots % 14
    owner_y, owner_xh, owner_z, owner_c = owner // 16, owner // 8 % 2, owner // 2 % 4, owner % 2
    handler = k // 7
    ahead_y, ahead_z = (owner_y - y) % 4, (owner_z - z) % 4
    first = jnp.where(handler == 0, ahead_y, ahead_z)
    second = jnp.where(handler == 0, ahead_z, ahead_y)
    over_x = (owner_xh + xh) % 2
    kept = jnp.where(handler == 0, (over_x + frame) % 2, over_x) == 0

    def start(prefix, size):
        at0, at2, at13 = (PIECES[prefix + ring][0] for ring in ("0", "2", "13"))
        return jnp.where(first == 0, at0, jnp.where(first == 2, at2, at13 + size * (first // 2)))

    plain = start("plain", 56) + (second * 2 + over_x) * 7
    halved = jnp.where(kept, start("kept", 28), start("given", 28)) + second * 7
    place = jnp.where(owner_c == handler, plain, halved) + k % 7
    return ((handler + core) % 2 * 448 + place).astype(jnp.int32)


def local(
    tokens,
    modulation,
    box_bounds,
    masters,
    left_stats,
    right_stats,
    left_roots,
    right_roots,
    owner_slot,
    cotangent,
):
    y, xh, z, core = (lax.axis_index(a) for a in POS)
    mine, copy = lax.axis_index(POS), lax.axis_index("frame")

    def to_frames(value):
        return lax.all_to_all(value.reshape(64, 4, D), POS, 0, 0, tiled=True).reshape(TOK, D)

    clip, frame = mine // 16, mine % 16
    bounds_here = lax.dynamic_index_in_dim(box_bounds, clip, 0, keepdims=False)
    box_first = jnp.concatenate([bounds_here, jnp.stack([frame, clip])]).astype(jnp.int32)
    box_second = jnp.concatenate([box_bounds.reshape(24), jnp.stack([mine * 4])]).astype(jnp.int32)
    where = source_of(owner_slot, y, xh, z, core)
    place = place_of(owner_slot, y, xh, z, core, copy)
    upstream = cotangent.reshape(TOK, D)
    tokens_here = to_frames(tokens)
    slots = gather_tiles(masters.astype(bf16), [tokens_here, where, place])
    middle, passed, *kept = run_first_forward(where, box_first, tokens_here, modulation, slots)
    here = to_frames(passed)
    block_output, grad_here, *grads = run_second(where, place, box_second, here, upstream, modulation, slots)
    upstream = to_frames(grad_here)
    token_grads, *grads = run_first_backward(
        where, place, box_first, tokens_here, middle, upstream, modulation, slots, kept, grads
    )
    slot_ids = mine * 14 + jnp.arange(14, dtype=jnp.int32)
    holds = jnp.any(owner_slot[None, :] == slot_ids[:, None], axis=1)
    sources = [masters, left_stats, right_stats, left_roots, right_roots]

    def info(start):
        return jnp.concatenate([jnp.stack([start]), holds]).astype(jnp.int32)

    def renew(terms):
        return run_precondition(info(core * 7), terms, sources, [])

    renewed, halved, token_grads = reduce_tiles(grads[:3], grads[3:], core, copy, token_grads, to_frames, renew)
    renewed = run_precondition(info(7 - core * 7), [halved], sources, renewed)
    return (block_output.reshape(tokens.shape), token_grads.reshape(tokens.shape), *renewed)


def solution(mesh):
    split = Mesh(
        mesh.devices.reshape(4, 2, 4, 2, mesh.shape["frame"]),
        ("pos_0", "pos_1", "pos_2", "pos_3", "frame"),
    )
    return jax.shard_map(
        local,
        mesh=split,
        in_specs=(
            P("frame", None, POS, None),
            P("frame", None, None, None, None),
            P("frame", None),
            P(POS, None, None),
            P(POS, None, None),
            P(POS, None, None),
            P(POS, None, None),
            P(POS, None, None),
            P(),
            P("frame", None, POS, None),
        ),
        out_specs=(
            P("frame", None, POS, None),
            P("frame", None, POS, None),
            P(POS, None, None),
            P(POS, None, None),
            P(POS, None, None),
            P(POS, None, None),
        ),
        check_vma=False,
    )
```
